32 devices in a mesh: det: 4 (over y, x), tm: 8 (over z, core).
Axes of the slice: x: 2, y: 2, z: 4, core: 2. Of those that a mesh axis runs over, the one named last changes fastest.
Arguments:
- tod: float32 [64, 32768], P('det', 'tm'), may hold values from -6 to 6
- pointing: int32 [64, 32768], P('det', 'tm'), may hold values from 0 to 1535
- noise_level: float32 [4, 64], P(None, 'det'), may hold values from 0.5 to 4
- modes: float32 [4, 64, 128], P(None, 'det'), may hold values from -2 to 2
Outputs:
- filtered: float32 [64, 32768], P('det', 'tm')
- binned: float32 [1536], P(('det', 'tm'))
The draws below stay inside these ranges and needn't reach their ends.
All inputs are finite; a program needn't handle non-finite values.
Results may differ from the reference program's by a relative error of at most 0.00026.
Values sent between devices are 32-bit elements; how exact they have to be, the bound alone decides.
A program may use at most 64 MiB of HBM per device.

```python
import math
import jax
import jax.numpy as jnp
from jax import lax

MODES = 128
NS = 32768
ND = 64
NB = 4
NPIX = 1536


def draw_pointing(key, part):
    subkeys = jax.random.split(key, 6)
    half_width = jax.random.randint(subkeys[0], (ND, 1), NS // 32, NS // 8 + 1)
    scan_speed = jax.random.randint(subkeys[1], (ND, 1), 1, 4)
    sweep_phase = jax.random.randint(subkeys[2], (ND, 1), 0, 1 << 20) % (4 * half_width)
    drift_rate = jax.random.randint(subkeys[3], (ND, 1), 0, 1 << 20) % (half_width + 1)
    left_draw = jax.random.randint(subkeys[4], (ND, 1), 0, NPIX)
    right_draw = jax.random.randint(subkeys[5], (ND, 1), 0, NPIX)
    start_pixel = (left_draw + right_draw) // 2 - half_width
    detector_index = jnp.arange(ND, dtype=jnp.int32)[:, None]
    start_pixel = jnp.where(detector_index == 0, -half_width, start_pixel)
    start_pixel = jnp.where(detector_index == ND - 1, NPIX - 1 - half_width, start_pixel)
    sample_index = jnp.arange(NS, dtype=jnp.int32)[None, :]
    sweep_period = 4 * half_width
    sweep_offset = jnp.abs((sample_index * scan_speed + sweep_phase) % sweep_period - 2 * half_width)
    drift_offset = sample_index * drift_rate // NS
    return jnp.clip(start_pixel + sweep_offset + drift_offset, 0, NPIX - 1).astype(jnp.int32)


def block_scale(key, dims, cuts, low, high):
    gain, own = 1.0, jax.random.fold_in(key, 6)
    for position, blocks in cuts:
        heights = jnp.exp(jax.random.uniform(jax.random.fold_in(own, position), (blocks,), jnp.float32, low / len(cuts), high / len(cuts)))
        gain = gain * jnp.repeat(heights, dims[position] // blocks).reshape([-1 if axis == position else 1 for axis in range(len(dims))])
    return gain


def gaussian(stream_key, dims, deviation, bound, cuts=(), held_as=jnp.bfloat16):
    loudness = block_scale(stream_key, dims, cuts, -0.22, 0.18) if cuts else 1.0
    entries = jax.random.normal(stream_key, dims, jnp.float32) * deviation * loudness
    return jnp.minimum(jnp.maximum(entries, -bound), bound).astype(held_as)


def setup_inputs(seed: int = 0) -> dict:
    arg_keys = jax.random.split(jax.random.key(seed), 5)
    tod = gaussian(arg_keys[0], (ND, NS), 1.0, 6.0, ((0, 4), (1, 8)), jnp.float32)
    pointing = draw_pointing(jax.random.fold_in(arg_keys[4], 71), 0)
    noise_level = jnp.clip(jnp.exp(math.log(4.0) - 2.0794415 * jax.random.uniform(arg_keys[2], (NB, ND), jnp.float32) ** block_scale(arg_keys[2], (NB, ND), ((1, 4),), -0.2, 0.2)), 0.5, 4.0)
    modes = gaussian(arg_keys[3], (NB, ND, MODES), (ND // 8) ** -0.5, 2.0, ((1, 4),), jnp.float32)
    return dict(tod=tod, pointing=pointing, noise_level=noise_level, modes=modes)


def reference(tod, pointing, noise_level, modes):
    high = lax.Precision.HIGHEST
    width = NS // (2 * NB)
    spectrum = jnp.fft.rfft(tod, axis=1)
    spec_real = jnp.real(spectrum).astype(jnp.float32)
    spec_imag = jnp.imag(spectrum).astype(jnp.float32)
    eye = jnp.eye(MODES, dtype=jnp.float32)
    parts_real = []
    parts_imag = []
    for band in range(NB):
        low = band * width
        high_end = (band + 1) * width if band < NB - 1 else NS // 2 + 1
        count = high_end - low
        inverse = 1.0 / noise_level[band]
        basis = modes[band]
        gram = eye + jnp.dot(basis.T.astype(jnp.float32), (basis * inverse[:, None]).astype(jnp.float32), precision=high, preferred_element_type=jnp.float32)
        weighted = jnp.concatenate([spec_real[:, low:high_end], spec_imag[:, low:high_end]], axis=1) * inverse[:, None]
        proj = jnp.dot(basis.T.astype(jnp.float32), weighted.astype(jnp.float32), precision=high, preferred_element_type=jnp.float32)
        coef = jnp.linalg.solve(gram, proj)
        result = weighted - jnp.dot(basis.astype(jnp.float32), coef.astype(jnp.float32), precision=high, preferred_element_type=jnp.float32) * inverse[:, None]
        parts_real.append(result[:, :count])
        parts_imag.append(result[:, count:])
    full_real = jnp.concatenate(parts_real, axis=1)
    full_imag = jnp.concatenate(parts_imag, axis=1)
    filtered = jnp.fft.irfft(lax.complex(full_real, full_imag), n=NS, axis=1).astype(jnp.float32)
    sums = jax.ops.segment_sum(filtered.reshape(-1), pointing.reshape(-1), num_segments=NPIX)
    hits = jax.ops.segment_sum(jnp.ones((ND * NS,), jnp.float32), pointing.reshape(-1), num_segments=NPIX)
    binned = sums / jnp.sqrt(1.0 + hits)
    return (filtered, binned)
```

```python
import functools
import math

import jax
import jax.numpy as jnp
import numpy as np
from jax import lax
from jax.experimental import pallas as pl
from jax.experimental.pallas import tpu as pltpu
from jax.sharding import PartitionSpec as P

FA = 128
FB = 256
TPIX = 48


HIGHEST = lax.Precision.HIGHEST


def rotation_table(size, total, sign):
    index = jnp.arange(size, dtype=jnp.int32)
    product = index[:, None] * index[None, :] % total
    angle = 2.0 * math.pi / total * product.astype(jnp.float32)
    return (jnp.cos(angle), sign * jnp.sin(angle))


def transform(real_in, imag_in, rows, cols, sign, real_out):
    length = rows * cols
    count = real_in.shape[0]
    first_cos, first_sin = rotation_table(rows, rows, sign)
    last_cos, last_sin = rotation_table(cols, cols, sign)
    grid_real = real_in.reshape(count, rows, cols)
    section_real = jnp.einsum("jm,rmq->rjq", first_cos, grid_real, precision=HIGHEST)
    section_imag = jnp.einsum("jm,rmq->rjq", first_sin, grid_real, precision=HIGHEST)
    if imag_in is not None:
        grid_imag = imag_in.reshape(count, rows, cols)
        section_real = section_real - jnp.einsum(
            "jm,rmq->rjq", first_sin, grid_imag, precision=HIGHEST
        )
        section_imag = section_imag + jnp.einsum(
            "jm,rmq->rjq", first_cos, grid_imag, precision=HIGHEST
        )
    row_index = jnp.arange(rows, dtype=jnp.int32)
    col_index = jnp.arange(cols, dtype=jnp.int32)
    turn = (row_index[:, None] * col_index[None, :] % length).astype(jnp.float32) * (
        2.0 * math.pi / length
    )
    turn_cos = jnp.cos(turn)
    turn_sin = sign * jnp.sin(turn)
    mixed_real = section_real * turn_cos - section_imag * turn_sin
    mixed_imag = section_real * turn_sin + section_imag * turn_cos
    out_real = jnp.einsum("km,rjm->rkj", last_cos, mixed_real, precision=HIGHEST) - jnp.einsum(
        "km,rjm->rkj", last_sin, mixed_imag, precision=HIGHEST
    )
    if real_out:
        return out_real.reshape(count, length)
    out_imag = jnp.einsum("km,rjm->rkj", last_sin, mixed_real, precision=HIGHEST) + jnp.einsum(
        "km,rjm->rkj", last_cos, mixed_imag, precision=HIGHEST
    )
    return (out_real.reshape(count, length), out_imag.reshape(count, length))


def solve_modes(factor, rhs):
    lower_part = lax.linalg.triangular_solve(factor, rhs, left_side=True, lower=True)
    return lax.linalg.triangular_solve(
        factor, lower_part, left_side=True, lower=True, transpose_a=True
    )


def band_of(freq, length, width, bands):
    folded = jnp.minimum(freq, length - freq)
    return jnp.minimum(folded // width, bands - 1)


def pick(array, index):
    return lax.dynamic_index_in_dim(array, index, 0, keepdims=False)


def general_body(tod, pointing, noise_level, modes):
    groups = lax.axis_size("tm")
    row_pos = lax.axis_index("tm")
    det_dev, block = tod.shape
    det_row = det_dev // groups
    length = block * groups
    bands = noise_level.shape[0]
    width = length // groups
    half_block = length // (2 * groups)
    mode_count = modes.shape[2]
    eye = jnp.eye(mode_count, dtype=jnp.float32)
    start = row_pos * half_block
    main_band = band_of(start, length, width, bands)
    side_band = jnp.int32(bands - 1)
    scaled = modes / noise_level[:, :, None]
    partial_all = jnp.einsum("bdm,bdn->bmn", modes, scaled, precision=HIGHEST)
    summed = lax.psum(partial_all, "det")
    gram_main = pick(summed, main_band) + eye
    gram_side = pick(summed, side_band) + eye
    factor_main = jnp.linalg.cholesky(gram_main)
    factor_side = jnp.linalg.cholesky(gram_side)
    arranged = tod.reshape(groups, det_row, block)
    spec_real, spec_imag = transform(
        lax.all_to_all(arranged, "tm", split_axis=0, concat_axis=2, tiled=True)[0],
        None,
        FA,
        FB,
        -1.0,
        False,
    )
    spec_real, spec_imag = (spec_real[None], spec_imag[None])
    spec_real = spec_real[0]
    spec_imag = spec_imag[0]
    basis_main = pick(modes, main_band)
    inverse_main = 1.0 / pick(noise_level, main_band)
    basis_side = pick(modes, side_band)
    inverse_side = 1.0 / pick(noise_level, side_band)
    half = length // 2
    row_noise = lax.dynamic_slice_in_dim(inverse_side, row_pos * det_row, det_row)
    row_basis = lax.dynamic_slice_in_dim(basis_side, row_pos * det_row, det_row, 0)
    top_weighted = spec_real[:, half] * row_noise
    top_proj = jnp.dot(
        top_weighted, row_basis, precision=HIGHEST, preferred_element_type=jnp.float32
    )
    top_proj = lax.psum(top_proj, ("det", "tm"))
    band_real, band_imag = (
        lax.all_to_all(spec_real[:, :half], "tm", split_axis=1, concat_axis=0, tiled=True),
        lax.all_to_all(spec_imag[:, :half], "tm", split_axis=1, concat_axis=0, tiled=True),
    )
    stacked = jnp.concatenate([band_real, band_imag], axis=1) * inverse_main[:, None]
    proj_main = jnp.dot(
        basis_main.T, stacked, precision=HIGHEST, preferred_element_type=jnp.float32
    )
    proj_main = lax.psum(proj_main, "det")
    coef_main = solve_modes(factor_main, proj_main)
    out_main = (
        stacked
        - jnp.dot(basis_main, coef_main, precision=HIGHEST, preferred_element_type=jnp.float32)
        * inverse_main[:, None]
    )
    top_coef = solve_modes(factor_side, top_proj[:, None])[:, 0]
    top_out = (
        top_weighted
        - jnp.dot(row_basis, top_coef, precision=HIGHEST, preferred_element_type=jnp.float32)
        * row_noise
    )
    rows_real, rows_imag = (
        lax.all_to_all(out_main[:, :half_block], "tm", split_axis=0, concat_axis=1, tiled=True),
        lax.all_to_all(out_main[:, half_block:], "tm", split_axis=0, concat_axis=1, tiled=True),
    )
    full_real = jnp.concatenate(
        [rows_real, top_out[:, None], jnp.flip(rows_real[:, 1:], axis=1)], axis=1
    )
    full_imag = jnp.concatenate(
        [rows_imag, jnp.zeros((det_row, 1), jnp.float32), -jnp.flip(rows_imag[:, 1:], axis=1)],
        axis=1,
    )
    filtered_rows = transform(full_real, full_imag, FB, FA, 1.0, True) * (1.0 / length)
    filtered = lax.all_to_all(filtered_rows, "tm", split_axis=1, concat_axis=0, tiled=True)
    pixels = TPIX * lax.axis_size("det") * groups
    flat_pointing = pointing.reshape(-1)
    sums = jax.ops.segment_sum(filtered.reshape(-1), flat_pointing, num_segments=pixels)
    hits = jax.ops.segment_sum(
        jnp.ones(flat_pointing.shape, jnp.float32), flat_pointing, num_segments=pixels
    )
    sums, hits = (
        lax.psum_scatter(sums, ("det", "tm"), scatter_dimension=0, tiled=True),
        lax.psum_scatter(hits, ("det", "tm"), scatter_dimension=0, tiled=True),
    )
    return (filtered, sums / jnp.sqrt(1.0 + hits))


N1 = 128
N2 = 256
CHUNKS = 32
MESH = pl.DeviceIdType.MESH
NT = (((1,), (1,)), ((), ()))
NN = (((1,), (0,)), ((), ()))


def halves(table):
    table = np.asarray(table, np.float32)
    high = table.astype(jnp.bfloat16)
    low = (table - high.astype(np.float32)).astype(jnp.bfloat16)
    return np.stack([np.asarray(high), np.asarray(low)])


def tables():
    length = N1 * N2
    half = N1 // 2
    n1 = np.arange(N1)
    n2 = np.arange(N2)
    k1 = np.arange(half)
    angle = 2 * np.pi * (k1[:, None] * n1[None, :] % N1) / N1
    first = np.concatenate([np.cos(angle), -np.sin(angle)])
    first[half] = np.cos(np.pi * n1)
    turn = 2 * np.pi * (k1[:, None] * n2[None, :]) / length
    tc, ts = np.cos(turn), np.sin(turn)
    t1 = np.concatenate([tc, tc])
    t2 = np.concatenate([ts, -ts])
    t3 = np.concatenate([-ts, -ts])
    t4 = np.concatenate([tc, -tc])
    t1[0], t2[0], t3[0], t4[0] = 1.0, 0.0, 1.0, 0.0
    b = np.pi * n2 / N2
    t1[half], t2[half] = np.cos(b) + np.sin(b), 0.0
    t3[half], t4[half] = np.cos(b) - np.sin(b), 0.0
    twiddle = np.stack([t1, t2, t3, t4]).astype(np.float32)
    angle = 2 * np.pi * (n2[:, None] * n2[None, :] % N2) / N2
    last = np.concatenate([np.cos(angle), np.sin(angle)], axis=1)
    weight = np.full((N1,), 2.0 / length)
    weight[0] = weight[half] = 1.0 / length
    return (
        halves(first),
        twiddle,
        halves(last),
        halves(last.T),
        np.ascontiguousarray(np.swapaxes(twiddle, 1, 2)),
        halves(first.T * weight[None, :]),
    )


def split(x):
    high = x.astype(jnp.bfloat16)
    return high, (x - high.astype(jnp.float32)).astype(jnp.bfloat16)


def dot(a, b, dims):
    return lax.dot_general(a, b, dims, preferred_element_type=jnp.float32)


def dot3(a, b, dims):
    return dot(a[0], b[0], dims) + dot(a[0], b[1], dims) + dot(a[1], b[0], dims)


def invert_pair(matrix):
    size, lanes = matrix.shape
    row = lax.broadcasted_iota(jnp.int32, (size, lanes), 0)
    lane = lax.broadcasted_iota(jnp.int32, (size, lanes), 1)
    left = lane < size
    column = jnp.where(left, lane, lane - size)

    def step(k, a):
        at_row = row == k
        at_col = column == k
        picked = jnp.where(at_col, a, 0.0)
        one = jnp.sum(jnp.where(left, picked, 0.0), axis=1, keepdims=True)
        two = jnp.sum(jnp.where(left, 0.0, picked), axis=1, keepdims=True)
        c = jnp.where(left, one, two)
        pivot = jnp.sum(jnp.where(at_row, c, 0.0), axis=0, keepdims=True)
        r = jnp.sum(jnp.where(at_row, jnp.where(at_col, 1.0, a), 0.0), axis=0, keepdims=True)
        r = r * (1.0 / pivot)
        base = jnp.where(at_row | at_col, 0.0, a)
        return base - jnp.where(at_row, -1.0, c) * r

    return lax.fori_loop(0, size, step, matrix)


def expand(matrix):
    size = matrix.shape[0]
    big = size * 8
    spread = (
        lax.broadcasted_iota(jnp.int32, (big, size), 0) // 8
        == lax.broadcasted_iota(jnp.int32, (big, size), 1)
    )
    spread = jnp.where(spread, 1.0, 0.0).astype(jnp.bfloat16)
    same = (
        lax.broadcasted_iota(jnp.int32, (big, big), 0) % 8
        == lax.broadcasted_iota(jnp.int32, (big, big), 1) % 8
    )
    out = []
    for part in split(matrix):
        tall = dot(spread, part, NN).astype(jnp.bfloat16)
        wide = dot(tall, spread, NT)
        out.append(jnp.where(same, wide, 0.0).astype(jnp.bfloat16))
    return out


def fused(
    groups,
    dets,
    tod_ref,
    owner_ref,
    inside_ref,
    mode_ref,
    noise_ref,
    first_ref,
    twiddle_ref,
    last_ref,
    last_t_ref,
    twiddle_t_ref,
    first_t_ref,
    out_ref,
    map_ref,
    x_in,
    modes_all,
    noise_all,
    spec_send,
    spec_recv,
    back_send,
    back_recv,
    time_send,
    kron,
    map_send,
    map_recv,
    mode_sems,
    noise_sems,
    tod_sems,
    spec_sems,
    back_sems,
    time_sems,
    map_sems,
):
    i = lax.axis_index("det")
    t = lax.axis_index("tm")
    total = groups * dets
    me = i * groups + t
    chunk = t * dets + i
    per = mode_ref.shape[1]

    def place(p):
        q = p // groups
        return q, p - q * groups

    barrier = pltpu.get_barrier_semaphore()

    def greet(j, carry):
        q, u = place(lax.rem(me + j, total))
        pl.semaphore_signal(barrier, inc=1, device_id=(q, u), device_id_type=MESH)
        return carry

    lax.fori_loop(1, total, greet, 0)
    pl.semaphore_wait(barrier, total - 1)

    def remote(src, dst, sems, j, where):
        return pltpu.make_async_remote_copy(
            src_ref=src,
            dst_ref=dst,
            send_sem=sems.at[0, j],
            recv_sem=sems.at[1, j],
            device_id=where,
            device_id_type=MESH,
        )

    def mode_copy(j):
        rows = pl.ds(pl.multiple_of(i * per, per), per)
        return remote(
            mode_ref, modes_all.at[:, rows, :], mode_sems, j, (lax.rem(i + j, dets), t)
        )

    def noise_copy(j):
        rows = pl.ds(pl.multiple_of(i * per, per), per)
        return remote(
            noise_ref, noise_all.at[:, rows, :], noise_sems, j, (lax.rem(i + j, dets), t)
        )

    def tod_copy(j):
        u = lax.rem(t + j, groups)
        rows = pl.ds(pl.multiple_of(t * 16, 16), 16)
        return remote(tod_ref.at[u], x_in.at[:, rows, :], tod_sems, j, (i, u))

    def spec_copy(j):
        q, u = place(lax.rem(me + j, total))
        return remote(spec_send.at[u * dets + q], spec_recv.at[me], spec_sems, j, (q, u))

    def back_copy(j):
        p = lax.rem(me + j, total)
        return remote(back_send.at[p], back_recv.at[chunk], back_sems, j, place(p))

    def time_copy(j):
        u = lax.rem(t + j, groups)
        rows = pl.ds(pl.multiple_of(u * 16, 16), 16)
        return remote(time_send.at[:, rows, :], out_ref.at[t], time_sems, j, (i, u))

    def map_copy(j):
        p = lax.rem(me + j, total)
        return remote(map_send.at[p], map_recv.at[me], map_sems, j, place(p))

    def start_all(make, count):
        def go(j, carry):
            make(j).start()
            return carry

        lax.fori_loop(1, count, go, 0)

    def wait_all(make, count):
        def go(j, carry):
            make(j).wait()
            return carry

        lax.fori_loop(1, count, go, 0)

    start_all(mode_copy, dets)
    start_all(noise_copy, dets)
    start_all(tod_copy, groups)

    own_rows = pl.ds(pl.multiple_of(i * per, per), per)
    modes_all[:, own_rows, :] = mode_ref[...]
    noise_all[:, own_rows, :] = noise_ref[...]
    x_in[:, pl.ds(pl.multiple_of(t * 16, 16), 16), :] = tod_ref[t]
    wait_all(mode_copy, dets)
    wait_all(noise_copy, dets)

    count = modes_all.shape[1]
    square = (count, count)
    diagonal = lax.broadcasted_iota(jnp.int32, square, 0) == lax.broadcasted_iota(
        jnp.int32, square, 1
    )
    sides = []
    for s in range(2):
        basis = modes_all[s]
        outer = lax.dot_general(
            basis, basis, NT, precision=HIGHEST, preferred_element_type=jnp.float32
        )
        sides.append(outer + jnp.where(diagonal, noise_all[s][:, :count], 0.0))
    inverse = invert_pair(jnp.concatenate(sides, axis=1))
    for s in range(2):
        parts = expand(inverse[:, s * count : (s + 1) * count])
        kron[s, 0] = parts[0]
        kron[s, 1] = parts[1]

    wait_all(tod_copy, groups)
    grid = jnp.concatenate([x_in[0], x_in[1]], axis=1)
    section = dot3((first_ref[0], first_ref[1]), split(grid), NN)
    swapped = jnp.concatenate([section[N1 // 2 :], section[: N1 // 2]], axis=0)
    rows = []
    for d in range(2):
        part = section[:, d * N2 : (d + 1) * N2]
        other = swapped[:, d * N2 : (d + 1) * N2]
        rows.append(
            jnp.concatenate(
                [
                    part * twiddle_ref[0] + other * twiddle_ref[1],
                    part * twiddle_ref[2] + other * twiddle_ref[3],
                ],
                axis=1,
            )
        )
    spectrum = dot3((last_ref[0], last_ref[1]), split(jnp.concatenate(rows, axis=0)), NT)
    for d in range(2):
        spec_send[:, d * 8 : (d + 1) * 8, :] = spectrum[:, d * N1 : (d + 1) * N1].reshape(
            CHUNKS, 8, N1
        )
    start_all(spec_copy, total)
    spec_recv[me] = spec_send[chunk]
    wait_all(spec_copy, total)

    data = split(spec_recv[...].reshape(total * 16, N1))
    main = dot3((kron[0, 0], kron[0, 1]), data, NN)
    side = dot3((kron[1, 0], kron[1, 1]), data, NN)
    shape = (total * 16, N1)
    edge = (lax.broadcasted_iota(jnp.int32, shape, 0) % 8 == 0) & (
        lax.broadcasted_iota(jnp.int32, shape, 1) == 0
    )
    apart = jnp.where((t > groups // 2) & (i == 0), 1, 0)
    edge = edge & (jnp.full(shape, apart, jnp.int32) == 1)
    back_send[...] = jnp.where(edge, side, main).reshape(total, 16, N1)
    start_all(back_copy, total)
    back_recv[chunk] = back_send[me]
    wait_all(back_copy, total)

    weighted = jnp.concatenate(
        [back_recv[:, d * 8 : (d + 1) * 8, :].reshape(N2, N1) for d in range(2)], axis=1
    )
    spread = dot3((last_t_ref[0], last_t_ref[1]), split(weighted), NN)
    upright = []
    for d in range(2):
        p = spread[:N2, d * N1 : (d + 1) * N1]
        q = spread[N2:, d * N1 : (d + 1) * N1]
        crossed = p * twiddle_t_ref[1] + q * twiddle_t_ref[3]
        upright.append(
            p * twiddle_t_ref[0]
            + q * twiddle_t_ref[2]
            + jnp.concatenate([crossed[:, N1 // 2 :], crossed[:, : N1 // 2]], axis=1)
        )
    stamped = dot3(
        (first_t_ref[0], first_t_ref[1]), split(jnp.concatenate(upright, axis=0)), NT
    )
    for d in range(2):
        time_send[d] = stamped[:, d * N2 : (d + 1) * N2]
    start_all(time_copy, groups)
    out_ref[t] = time_send[:, pl.ds(pl.multiple_of(t * 16, 16), 16), :]
    wait_all(time_copy, groups)

    width = 8 * N2
    own_index = lax.broadcasted_iota(jnp.int32, (total, width), 0)
    inside_index = lax.broadcasted_iota(jnp.int32, (TPIX, width), 0)

    def flat(block):
        return jnp.concatenate([block[r : r + 1] for r in range(8)], axis=1)

    def bin_rows(g, acc):
        a = g // 4
        b = g - a * 4
        c = b // 2
        rows = pl.ds(pl.multiple_of((b - c * 2) * 8, 8), 8)
        high, low = split(flat(out_ref[a, c, rows, :]))
        mine = jnp.broadcast_to(flat(owner_ref[a, c, rows, :]), (total, width)) == own_index
        spot = jnp.broadcast_to(flat(inside_ref[a, c, rows, :]), (TPIX, width)) == inside_index
        high = jnp.where(mine, jnp.broadcast_to(high.astype(jnp.float32), (total, width)), 0.0)
        low = jnp.where(mine, jnp.broadcast_to(low.astype(jnp.float32), (total, width)), 0.0)
        ones = jnp.where(mine, 1.0, 0.0)
        lhs = jnp.concatenate([high, low, ones], axis=0).astype(jnp.bfloat16)
        rhs = jnp.where(spot, 1.0, 0.0).astype(jnp.bfloat16)
        return acc + dot(lhs, rhs, NT)

    acc = lax.fori_loop(0, 4 * groups, bin_rows, jnp.zeros((3 * total, TPIX), jnp.float32))
    acc = jnp.concatenate([acc, jnp.zeros((3 * total, 128 - TPIX), jnp.float32)], axis=1)
    map_send[...] = jnp.zeros(map_send.shape, jnp.float32)
    map_send[:, 0, :] = acc[:total] + acc[total : 2 * total]
    map_send[:, 1, :] = acc[2 * total :]
    start_all(map_copy, total)
    map_recv[me] = map_send[me]
    wait_all(map_copy, total)
    summed = jnp.sum(map_recv[...], axis=0)
    map_ref[...] = jnp.broadcast_to(summed[0:1] / jnp.sqrt(1.0 + summed[1:2]), map_ref.shape)


def fast_body(tod, pointing, noise_level, modes):
    groups = lax.axis_size("tm")
    dets = lax.axis_size("det")
    t = lax.axis_index("tm")
    det_dev = tod.shape[0]
    bands = noise_level.shape[0]
    total = groups * dets
    main_band = jnp.minimum(t, groups - 1 - t)
    side_band = jnp.minimum(main_band + 1, bands - 1)
    blocks = (groups, det_dev // groups, 16, N2)
    owner = (pointing // TPIX).reshape(blocks)
    inside = (pointing % TPIX).reshape(blocks)
    pair_modes = jnp.stack([pick(modes, main_band), pick(modes, side_band)])
    pair_noise = jnp.stack([pick(noise_level, main_band), pick(noise_level, side_band)])
    pair_noise = jnp.broadcast_to(pair_noise[:, :, None], pair_modes.shape)
    everyone = det_dev * dets
    f32 = jnp.float32
    constants = [jnp.asarray(c) for c in tables()]
    vmem = pl.BlockSpec(memory_space=pltpu.VMEM)
    out, binned = pl.pallas_call(
        functools.partial(fused, groups, dets),
        out_shape=(
            jax.ShapeDtypeStruct(blocks, f32),
            jax.ShapeDtypeStruct((8, 128), f32),
        ),
        in_specs=[vmem] * (5 + len(constants)),
        out_specs=(vmem, vmem),
        scratch_shapes=[
            pltpu.VMEM((2, N1, N2), f32),
            pltpu.VMEM((2, everyone, 128), f32),
            pltpu.VMEM((2, everyone, 128), f32),
            pltpu.VMEM((total, 16, 128), f32),
            pltpu.VMEM((total, 16, 128), f32),
            pltpu.VMEM((total, 16, 128), f32),
            pltpu.VMEM((total, 16, 128), f32),
            pltpu.VMEM((2, N1, N2), f32),
            pltpu.VMEM((2, 2, everyone * 8, everyone * 8), jnp.bfloat16),
            pltpu.VMEM((total, 8, 128), f32),
            pltpu.VMEM((total, 8, 128), f32),
            pltpu.SemaphoreType.DMA((2, dets)),
            pltpu.SemaphoreType.DMA((2, dets)),
            pltpu.SemaphoreType.DMA((2, groups)),
            pltpu.SemaphoreType.DMA((2, total)),
            pltpu.SemaphoreType.DMA((2, total)),
            pltpu.SemaphoreType.DMA((2, groups)),
            pltpu.SemaphoreType.DMA((2, total)),
        ],
        compiler_params=pltpu.CompilerParams(
            collective_id=0, has_side_effects=True, vmem_limit_bytes=40 * 1024 * 1024
        ),
    )(tod.reshape(blocks), owner, inside, pair_modes, pair_noise, *constants)
    return out.reshape(tod.shape), binned[0, :TPIX]


def body(tod, pointing, noise_level, modes):
    groups = lax.axis_size("tm")
    dets = lax.axis_size("det")
    fits = (
        groups * dets == CHUNKS
        and groups == 2 * noise_level.shape[0]
        and tod.shape == (2 * groups, N1 * N2 // groups)
        and modes.shape[2] == 128
        and 16 * groups == N1
    )
    return (fast_body if fits else general_body)(tod, pointing, noise_level, modes)


def solution(mesh):
    placed = (P("det", "tm"), P("det", "tm"), P(None, "det"), P(None, "det", None))
    return jax.shard_map(
        body,
        mesh=mesh,
        in_specs=placed,
        out_specs=(P("det", "tm"), P(("det", "tm"))),
        check_vma=False,
    )
```

```python
import functools
import math

import jax
import jax.numpy as jnp
import numpy as np
from jax import lax
from jax.experimental import pallas as pl
from jax.experimental.pallas import tpu as pltpu
from jax.sharding import PartitionSpec as P

FA = 128
FB = 256
TPIX = 48


HIGHEST = lax.Precision.HIGHEST


def rotation_table(size, total, sign):
    index = jnp.arange(size, dtype=jnp.int32)
    product = index[:, None] * index[None, :] % total
    angle = 2.0 * math.pi / total * product.astype(jnp.float32)
    return (jnp.cos(angle), sign * jnp.sin(angle))


def transform(real_in, imag_in, rows, cols, sign, real_out):
    length = rows * cols
    count = real_in.shape[0]
    first_cos, first_sin = rotation_table(rows, rows, sign)
    last_cos, last_sin = rotation_table(cols, cols, sign)
    grid_real = real_in.reshape(count, rows, cols)
    section_real = jnp.einsum("jm,rmq->rjq", first_cos, grid_real, precision=HIGHEST)
    section_imag = jnp.einsum("jm,rmq->rjq", first_sin, grid_real, precision=HIGHEST)
    if imag_in is not None:
        grid_imag = imag_in.reshape(count, rows, cols)
        section_real = section_real - jnp.einsum(
            "jm,rmq->rjq", first_sin, grid_imag, precision=HIGHEST
        )
        section_imag = section_imag + jnp.einsum(
            "jm,rmq->rjq", first_cos, grid_imag, precision=HIGHEST
        )
    row_index = jnp.arange(rows, dtype=jnp.int32)
    col_index = jnp.arange(cols, dtype=jnp.int32)
    turn = (row_index[:, None] * col_index[None, :] % length).astype(jnp.float32) * (
        2.0 * math.pi / length
    )
    turn_cos = jnp.cos(turn)
    turn_sin = sign * jnp.sin(turn)
    mixed_real = section_real * turn_cos - section_imag * turn_sin
    mixed_imag = section_real * turn_sin + section_imag * turn_cos
    out_real = jnp.einsum("km,rjm->rkj", last_cos, mixed_real, precision=HIGHEST) - jnp.einsum(
        "km,rjm->rkj", last_sin, mixed_imag, precision=HIGHEST
    )
    if real_out:
        return out_real.reshape(count, length)
    out_imag = jnp.einsum("km,rjm->rkj", last_sin, mixed_real, precision=HIGHEST) + jnp.einsum(
        "km,rjm->rkj", last_cos, mixed_imag, precision=HIGHEST
    )
    return (out_real.reshape(count, length), out_imag.reshape(count, length))


def solve_modes(factor, rhs):
    lower_part = lax.linalg.triangular_solve(factor, rhs, left_side=True, lower=True)
    return lax.linalg.triangular_solve(
        factor, lower_part, left_side=True, lower=True, transpose_a=True
    )


def band_of(freq, length, width, bands):
    folded = jnp.minimum(freq, length - freq)
    return jnp.minimum(folded // width, bands - 1)


def pick(array, index):
    return lax.dynamic_index_in_dim(array, index, 0, keepdims=False)


def general_body(tod, pointing, noise_level, modes):
    groups = lax.axis_size("tm")
    row_pos = lax.axis_index("tm")
    det_dev, block = tod.shape
    det_row = det_dev // groups
    length = block * groups
    bands = noise_level.shape[0]
    width = length // groups
    half_block = length // (2 * groups)
    mode_count = modes.shape[2]
    eye = jnp.eye(mode_count, dtype=jnp.float32)
    start = row_pos * half_block
    main_band = band_of(start, length, width, bands)
    side_band = jnp.int32(bands - 1)
    scaled = modes / noise_level[:, :, None]
    partial_all = jnp.einsum("bdm,bdn->bmn", modes, scaled, precision=HIGHEST)
    summed = lax.psum(partial_all, "det")
    gram_main = pick(summed, main_band) + eye
    gram_side = pick(summed, side_band) + eye
    factor_main = jnp.linalg.cholesky(gram_main)
    factor_side = jnp.linalg.cholesky(gram_side)
    arranged = tod.reshape(groups, det_row, block)
    spec_real, spec_imag = transform(
        lax.all_to_all(arranged, "tm", split_axis=0, concat_axis=2, tiled=True)[0],
        None,
        FA,
        FB,
        -1.0,
        False,
    )
    spec_real, spec_imag = (spec_real[None], spec_imag[None])
    spec_real = spec_real[0]
    spec_imag = spec_imag[0]
    basis_main = pick(modes, main_band)
    inverse_main = 1.0 / pick(noise_level, main_band)
    basis_side = pick(modes, side_band)
    inverse_side = 1.0 / pick(noise_level, side_band)
    half = length // 2
    row_noise = lax.dynamic_slice_in_dim(inverse_side, row_pos * det_row, det_row)
    row_basis = lax.dynamic_slice_in_dim(basis_side, row_pos * det_row, det_row, 0)
    top_weighted = spec_real[:, half] * row_noise
    top_proj = jnp.dot(
        top_weighted, row_basis, precision=HIGHEST, preferred_element_type=jnp.float32
    )
    top_proj = lax.psum(top_proj, ("det", "tm"))
    band_real, band_imag = (
        lax.all_to_all(spec_real[:, :half], "tm", split_axis=1, concat_axis=0, tiled=True),
        lax.all_to_all(spec_imag[:, :half], "tm", split_axis=1, concat_axis=0, tiled=True),
    )
    stacked = jnp.concatenate([band_real, band_imag], axis=1) * inverse_main[:, None]
    proj_main = jnp.dot(
        basis_main.T, stacked, precision=HIGHEST, preferred_element_type=jnp.float32
    )
    proj_main = lax.psum(proj_main, "det")
    coef_main = solve_modes(factor_main, proj_main)
    out_main = (
        stacked
        - jnp.dot(basis_main, coef_main, precision=HIGHEST, preferred_element_type=jnp.float32)
        * inverse_main[:, None]
    )
    top_coef = solve_modes(factor_side, top_proj[:, None])[:, 0]
    top_out = (
        top_weighted
        - jnp.dot(row_basis, top_coef, precision=HIGHEST, preferred_element_type=jnp.float32)
        * row_noise
    )
    rows_real, rows_imag = (
        lax.all_to_all(out_main[:, :half_block], "tm", split_axis=0, concat_axis=1, tiled=True),
        lax.all_to_all(out_main[:, half_block:], "tm", split_axis=0, concat_axis=1, tiled=True),
    )
    full_real = jnp.concatenate(
        [rows_real, top_out[:, None], jnp.flip(rows_real[:, 1:], axis=1)], axis=1
    )
    full_imag = jnp.concatenate(
        [rows_imag, jnp.zeros((det_row, 1), jnp.float32), -jnp.flip(rows_imag[:, 1:], axis=1)],
        axis=1,
    )
    filtered_rows = transform(full_real, full_imag, FB, FA, 1.0, True) * (1.0 / length)
    filtered = lax.all_to_all(filtered_rows, "tm", split_axis=1, concat_axis=0, tiled=True)
    pixels = TPIX * lax.axis_size("det") * groups
    flat_pointing = pointing.reshape(-1)
    sums = jax.ops.segment_sum(filtered.reshape(-1), flat_pointing, num_segments=pixels)
    hits = jax.ops.segment_sum(
        jnp.ones(flat_pointing.shape, jnp.float32), flat_pointing, num_segments=pixels
    )
    sums, hits = (
        lax.psum_scatter(sums, ("det", "tm"), scatter_dimension=0, tiled=True),
        lax.psum_scatter(hits, ("det", "tm"), scatter_dimension=0, tiled=True),
    )
    return (filtered, sums / jnp.sqrt(1.0 + hits))


N1 = 128
N2 = 256
CHUNKS = 32
UNROLL = 1
MESH = pl.DeviceIdType.MESH
NT = (((1,), (1,)), ((), ()))
NN = (((1,), (0,)), ((), ()))


def halves(table):
    table = np.asarray(table, np.float32)
    high = table.astype(jnp.bfloat16)
    low = (table - high.astype(np.float32)).astype(jnp.bfloat16)
    return np.stack([np.asarray(high), np.asarray(low)])


def tables():
    length = N1 * N2
    half = N1 // 2
    n1 = np.arange(N1)
    n2 = np.arange(N2)
    k1 = np.arange(half)
    angle = 2 * np.pi * (k1[:, None] * n1[None, :] % N1) / N1
    first = np.concatenate([np.cos(angle), -np.sin(angle)])
    first[half] = np.cos(np.pi * n1)
    turn = 2 * np.pi * (k1[:, None] * n2[None, :]) / length
    tc, ts = np.cos(turn), np.sin(turn)
    t1 = np.concatenate([tc, tc])
    t2 = np.concatenate([ts, -ts])
    t3 = np.concatenate([-ts, -ts])
    t4 = np.concatenate([tc, -tc])
    t1[0], t2[0], t3[0], t4[0] = 1.0, 0.0, 1.0, 0.0
    b = np.pi * n2 / N2
    t1[half], t2[half] = np.cos(b) + np.sin(b), 0.0
    t3[half], t4[half] = np.cos(b) - np.sin(b), 0.0
    twiddle = np.stack([t1, t2, t3, t4]).astype(np.float32)
    angle = 2 * np.pi * (n2[:, None] * n2[None, :] % N2) / N2
    last = np.concatenate([np.cos(angle), np.sin(angle)], axis=1)
    weight = np.full((N1,), 2.0 / length)
    weight[0] = weight[half] = 1.0 / length
    return (
        halves(first),
        twiddle,
        halves(last),
        halves(last.T),
        np.ascontiguousarray(np.swapaxes(twiddle, 1, 2)),
        halves(first.T * weight[None, :]),
    )


def split(x):
    high = x.astype(jnp.bfloat16)
    return high, (x - high.astype(jnp.float32)).astype(jnp.bfloat16)


def dot(a, b, dims):
    return lax.dot_general(a, b, dims, preferred_element_type=jnp.float32)


def dot3(a, b, dims):
    return dot(a[0], b[0], dims) + dot(a[0], b[1], dims) + dot(a[1], b[0], dims)


def invert_pair(matrix):
    size, lanes = matrix.shape
    row = lax.broadcasted_iota(jnp.int32, (size, lanes), 0)
    lane = lax.broadcasted_iota(jnp.int32, (size, lanes), 1)
    left = lane < size
    column = jnp.where(left, lane, lane - size)

    def step(k, a):
        at_row = row == k
        at_col = column == k
        picked = jnp.where(at_col, a, 0.0)
        one = jnp.sum(jnp.where(left, picked, 0.0), axis=1, keepdims=True)
        two = jnp.sum(jnp.where(left, 0.0, picked), axis=1, keepdims=True)
        c = jnp.where(left, one, two)
        pivot = jnp.sum(jnp.where(at_row, c, 0.0), axis=0, keepdims=True)
        r = jnp.sum(jnp.where(at_row, jnp.where(at_col, 1.0, a), 0.0), axis=0, keepdims=True)
        r = r * (1.0 / pivot)
        base = jnp.where(at_row | at_col, 0.0, a)
        return base - jnp.where(at_row, -1.0, c) * r

    return lax.fori_loop(0, size, step, matrix)


def expand(matrix):
    size = matrix.shape[0]
    big = size * 8
    spread = (
        lax.broadcasted_iota(jnp.int32, (big, size), 0) // 8
        == lax.broadcasted_iota(jnp.int32, (big, size), 1)
    )
    spread = jnp.where(spread, 1.0, 0.0).astype(jnp.bfloat16)
    same = (
        lax.broadcasted_iota(jnp.int32, (big, big), 0) % 8
        == lax.broadcasted_iota(jnp.int32, (big, big), 1) % 8
    )
    out = []
    for part in split(matrix):
        tall = dot(spread, part, NN).astype(jnp.bfloat16)
        wide = dot(tall, spread, NT)
        out.append(jnp.where(same, wide, 0.0).astype(jnp.bfloat16))
    return out


def fused(
    groups,
    dets,
    tod_ref,
    owner_ref,
    inside_ref,
    mode_ref,
    first_hbm,
    twiddle_hbm,
    last_hbm,
    last_t_hbm,
    twiddle_t_hbm,
    first_t_hbm,
    out_ref,
    map_ref,
    x_in,
    modes_all,
    spec_send,
    spec_recv,
    back_send,
    back_recv,
    time_send,
    kron,
    map_send,
    map_recv,
    first_ref,
    twiddle_ref,
    last_ref,
    last_t_ref,
    twiddle_t_ref,
    first_t_ref,
    masks,
    spots,
    load_sems,
    mode_sems,
    tod_sems,
    spec_sems,
    back_sems,
    time_sems,
    map_sems,
):
    i = lax.axis_index("det")
    t = lax.axis_index("tm")
    total = groups * dets
    me = i * groups + t
    chunk = t * dets + i
    per = mode_ref.shape[1]

    loads = [
        pltpu.make_async_copy(src, dst, load_sems.at[n])
        for n, (src, dst) in enumerate(
            [
                (first_hbm, first_ref),
                (twiddle_hbm, twiddle_ref),
                (last_hbm, last_ref),
                (last_t_hbm, last_t_ref),
                (twiddle_t_hbm, twiddle_t_ref),
                (first_t_hbm, first_t_ref),
            ]
        )
    ]

    def place(p):
        q = p // groups
        return q, p - q * groups

    barrier = pltpu.get_barrier_semaphore()

    def greet(j, carry):
        q, u = place(lax.rem(me + j, total))
        pl.semaphore_signal(barrier, inc=1, device_id=(q, u), device_id_type=MESH)
        return carry

    lax.fori_loop(1, total, greet, 0, unroll=UNROLL)
    for load in loads:
        load.start()
    pl.semaphore_wait(barrier, total - 1)

    def remote(src, dst, sems, j, where):
        return pltpu.make_async_remote_copy(
            src_ref=src,
            dst_ref=dst,
            send_sem=sems.at[0, j],
            recv_sem=sems.at[1, j],
            device_id=where,
            device_id_type=MESH,
        )

    def mode_copy(j):
        rows = pl.ds(pl.multiple_of(i * per, per), per)
        return remote(
            mode_ref, modes_all.at[:, rows, :], mode_sems, j, (lax.rem(i + j, dets), t)
        )

    def tod_copy(j):
        u = lax.rem(t + j, groups)
        rows = pl.ds(pl.multiple_of(t * 16, 16), 16)
        return remote(tod_ref.at[u], x_in.at[:, rows, :], tod_sems, j, (i, u))

    def spec_copy(j):
        q, u = place(lax.rem(me + j, total))
        return remote(spec_send.at[u * dets + q], spec_recv.at[me], spec_sems, j, (q, u))

    def back_copy(j):
        p = lax.rem(me + j, total)
        return remote(back_send.at[p], back_recv.at[chunk], back_sems, j, place(p))

    def time_copy(j):
        u = lax.rem(t + j, groups)
        rows = pl.ds(pl.multiple_of(u * 16, 16), 16)
        return remote(time_send.at[:, rows, :], out_ref.at[t], time_sems, j, (i, u))

    def map_copy(j):
        p = lax.rem(me + j, total)
        return remote(map_send.at[p], map_recv.at[me], map_sems, j, place(p))

    def start_all(make, count):
        def go(j, carry):
            make(j).start()
            return carry

        lax.fori_loop(1, count, go, 0, unroll=UNROLL)

    def wait_all(make, count):
        def go(j, carry):
            make(j).wait()
            return carry

        lax.fori_loop(1, count, go, 0, unroll=UNROLL)

    start_all(mode_copy, dets)
    start_all(tod_copy, groups)

    own_rows = pl.ds(pl.multiple_of(i * per, per), per)
    modes_all[:, own_rows, :] = mode_ref[...]
    x_in[:, pl.ds(pl.multiple_of(t * 16, 16), 16), :] = tod_ref[t]
    for load in loads:
        load.wait()
    wait_all(tod_copy, groups)
    grid = jnp.concatenate([x_in[0], x_in[1]], axis=1)
    section = dot3((first_ref[0], first_ref[1]), split(grid), NN)
    swapped = jnp.concatenate([section[N1 // 2 :], section[: N1 // 2]], axis=0)
    rows = []
    for d in range(2):
        part = section[:, d * N2 : (d + 1) * N2]
        other = swapped[:, d * N2 : (d + 1) * N2]
        rows.append(
            jnp.concatenate(
                [
                    part * twiddle_ref[0] + other * twiddle_ref[1],
                    part * twiddle_ref[2] + other * twiddle_ref[3],
                ],
                axis=1,
            )
        )
    spectrum = dot3((last_ref[0], last_ref[1]), split(jnp.concatenate(rows, axis=0)), NT)
    for d in range(2):
        spec_send[:, d * 8 : (d + 1) * 8, :] = spectrum[:, d * N1 : (d + 1) * N1].reshape(
            CHUNKS, 8, N1
        )
    start_all(spec_copy, total)
    spec_recv[me] = spec_send[chunk]
    wait_all(mode_copy, dets)

    count = modes_all.shape[1]
    square = (count, count)
    diagonal = lax.broadcasted_iota(jnp.int32, square, 0) == lax.broadcasted_iota(
        jnp.int32, square, 1
    )
    sides = []
    for s in range(2):
        basis = modes_all[s, :, :128]
        outer = lax.dot_general(
            basis, basis, NT, precision=HIGHEST, preferred_element_type=jnp.float32
        )
        sides.append(outer + jnp.where(diagonal, modes_all[s, :, 128 : 128 + count], 0.0))
    inverse = invert_pair(jnp.concatenate(sides, axis=1))
    for s in range(2):
        parts = expand(inverse[:, s * count : (s + 1) * count])
        kron[s, 0] = parts[0]
        kron[s, 1] = parts[1]

    wait_all(spec_copy, total)

    data = split(spec_recv[...].reshape(total * 16, N1))
    main = dot3((kron[0, 0], kron[0, 1]), data, NN)
    side = dot3((kron[1, 0], kron[1, 1]), data, NN)
    shape = (total * 16, N1)
    edge = (lax.broadcasted_iota(jnp.int32, shape, 0) % 8 == 0) & (
        lax.broadcasted_iota(jnp.int32, shape, 1) == 0
    )
    apart = jnp.where((t > groups // 2) & (i == 0), 1, 0)
    edge = edge & (jnp.full(shape, apart, jnp.int32) == 1)
    back_send[...] = jnp.where(edge, side, main).reshape(total, 16, N1)
    start_all(back_copy, total)
    back_recv[chunk] = back_send[me]

    width = 8 * N2
    own_index = lax.broadcasted_iota(jnp.int32, (total, width), 0)
    inside_index = lax.broadcasted_iota(jnp.int32, (TPIX, width), 0)

    def flat(block):
        return jnp.concatenate([block[r : r + 1] for r in range(8)], axis=1)

    def mark(g, acc):
        a = g // 4
        b = g - a * 4
        c = b // 2
        rows = pl.ds(pl.multiple_of((b - c * 2) * 8, 8), 8)
        mine = jnp.broadcast_to(flat(owner_ref[a, c, rows, :]), (total, width)) == own_index
        spot = jnp.broadcast_to(flat(inside_ref[a, c, rows, :]), (TPIX, width)) == inside_index
        mine = jnp.where(mine, 1.0, 0.0).astype(jnp.bfloat16)
        spot = jnp.where(spot, 1.0, 0.0).astype(jnp.bfloat16)
        masks[g] = mine
        spots[g] = spot
        return acc + dot(mine, spot, NT)

    hits = lax.fori_loop(0, 4 * groups, mark, jnp.zeros((total, TPIX), jnp.float32))
    wait_all(back_copy, total)

    weighted = jnp.concatenate(
        [back_recv[:, d * 8 : (d + 1) * 8, :].reshape(N2, N1) for d in range(2)], axis=1
    )
    spread = dot3((last_t_ref[0], last_t_ref[1]), split(weighted), NN)
    upright = []
    for d in range(2):
        p = spread[:N2, d * N1 : (d + 1) * N1]
        q = spread[N2:, d * N1 : (d + 1) * N1]
        crossed = p * twiddle_t_ref[1] + q * twiddle_t_ref[3]
        upright.append(
            p * twiddle_t_ref[0]
            + q * twiddle_t_ref[2]
            + jnp.concatenate([crossed[:, N1 // 2 :], crossed[:, : N1 // 2]], axis=1)
        )
    stamped = dot3(
        (first_t_ref[0], first_t_ref[1]), split(jnp.concatenate(upright, axis=0)), NT
    )
    for d in range(2):
        time_send[d] = stamped[:, d * N2 : (d + 1) * N2]
    start_all(time_copy, groups)
    out_ref[t] = time_send[:, pl.ds(pl.multiple_of(t * 16, 16), 16), :]

    def bin_block(a, acc):
        for b in range(4):
            values = out_ref[a, b // 2, b % 2 * 8 : b % 2 * 8 + 8, :]
            high, low = split(flat(values))
            mine = masks[a * 4 + b]
            lhs = jnp.concatenate(
                [
                    mine * jnp.broadcast_to(high, (total, width)),
                    mine * jnp.broadcast_to(low, (total, width)),
                ],
                axis=0,
            )
            acc = acc + dot(lhs, spots[a * 4 + b], NT)
        return acc

    def bin_arrived(j, acc):
        time_copy(j).wait()
        return bin_block(lax.rem(t - j + groups, groups), acc)

    acc = bin_block(t, jnp.zeros((2 * total, TPIX), jnp.float32))
    acc = lax.fori_loop(1, groups, bin_arrived, acc)
    pad = jnp.zeros((total, 128 - TPIX), jnp.float32)
    map_send[...] = jnp.zeros(map_send.shape, jnp.float32)
    map_send[:, 0, :] = jnp.concatenate([acc[:total] + acc[total:], pad], axis=1)
    map_send[:, 1, :] = jnp.concatenate([hits, pad], axis=1)
    start_all(map_copy, total)
    map_recv[me] = map_send[me]
    wait_all(map_copy, total)
    summed = jnp.sum(map_recv[...], axis=0)
    map_ref[...] = jnp.broadcast_to(summed[0:1] / jnp.sqrt(1.0 + summed[1:2]), map_ref.shape)


def fast_body(tod, pointing, noise_level, modes):
    groups = lax.axis_size("tm")
    dets = lax.axis_size("det")
    t = lax.axis_index("tm")
    det_dev = tod.shape[0]
    bands = noise_level.shape[0]
    total = groups * dets
    main_band = jnp.minimum(t, groups - 1 - t)
    side_band = jnp.minimum(main_band + 1, bands - 1)
    blocks = (groups, det_dev // groups, 16, N2)
    owner = (pointing // TPIX).reshape(blocks)
    inside = (pointing % TPIX).reshape(blocks)
    pair_modes = jnp.stack([pick(modes, main_band), pick(modes, side_band)])
    pair_noise = jnp.stack([pick(noise_level, main_band), pick(noise_level, side_band)])
    pair_noise = jnp.broadcast_to(pair_noise[:, :, None], pair_modes.shape)
    pair = jnp.concatenate([pair_modes, pair_noise], axis=2)
    everyone = det_dev * dets
    f32 = jnp.float32
    constants = [jnp.asarray(c) for c in tables()]
    vmem = pl.BlockSpec(memory_space=pltpu.VMEM)
    out, binned = pl.pallas_call(
        functools.partial(fused, groups, dets),
        out_shape=(
            jax.ShapeDtypeStruct(blocks, f32),
            jax.ShapeDtypeStruct((8, 128), f32),
        ),
        in_specs=[vmem] * 4 + [pl.BlockSpec(memory_space=pltpu.HBM)] * len(constants),
        out_specs=(vmem, vmem),
        scratch_shapes=[
            pltpu.VMEM((2, N1, N2), f32),
            pltpu.VMEM((2, everyone, 256), f32),
            pltpu.VMEM((total, 16, 128), f32),
            pltpu.VMEM((total, 16, 128), f32),
            pltpu.VMEM((total, 16, 128), f32),
            pltpu.VMEM((total, 16, 128), f32),
            pltpu.VMEM((2, N1, N2), f32),
            pltpu.VMEM((2, 2, everyone * 8, everyone * 8), jnp.bfloat16),
            pltpu.VMEM((total, 8, 128), f32),
            pltpu.VMEM((total, 8, 128), f32),
            *[pltpu.VMEM(c.shape, c.dtype) for c in constants],
            pltpu.VMEM((4 * groups, total, 8 * N2), jnp.bfloat16),
            pltpu.VMEM((4 * groups, TPIX, 8 * N2), jnp.bfloat16),
            pltpu.SemaphoreType.DMA((len(constants),)),
            pltpu.SemaphoreType.DMA((2, dets)),
            pltpu.SemaphoreType.DMA((2, groups)),
            pltpu.SemaphoreType.DMA((2, total)),
            pltpu.SemaphoreType.DMA((2, total)),
            pltpu.SemaphoreType.DMA((2, groups)),
            pltpu.SemaphoreType.DMA((2, total)),
        ],
        compiler_params=pltpu.CompilerParams(
            collective_id=0, has_side_effects=True, vmem_limit_bytes=40 * 1024 * 1024
        ),
    )(tod.reshape(blocks), owner, inside, pair, *constants)
    return out.reshape(tod.shape), binned[0, :TPIX]


def body(tod, pointing, noise_level, modes):
    groups = lax.axis_size("tm")
    dets = lax.axis_size("det")
    fits = (
        groups * dets == CHUNKS
        and groups == 2 * noise_level.shape[0]
        and tod.shape == (2 * groups, N1 * N2 // groups)
        and modes.shape[2] == 128
        and 16 * groups == N1
    )
    return (fast_body if fits else general_body)(tod, pointing, noise_level, modes)


def solution(mesh):
    placed = (P("det", "tm"), P("det", "tm"), P(None, "det"), P(None, "det", None))
    return jax.shard_map(
        body,
        mesh=mesh,
        in_specs=placed,
        out_specs=(P("det", "tm"), P(("det", "tm"))),
        check_vma=False,
    )
```

```python
import functools
import math

import jax
import jax.numpy as jnp
import numpy as np
from jax import lax
from jax.experimental import pallas as pl
from jax.experimental.pallas import tpu as pltpu
from jax.sharding import PartitionSpec as P

FA = 128
FB = 256
TPIX = 48


HIGHEST = lax.Precision.HIGHEST


def rotation_table(size, total, sign):
    index = jnp.arange(size, dtype=jnp.int32)
    product = index[:, None] * index[None, :] % total
    angle = 2.0 * math.pi / total * product.astype(jnp.float32)
    return (jnp.cos(angle), sign * jnp.sin(angle))


def transform(real_in, imag_in, rows, cols, sign, real_out):
    length = rows * cols
    count = real_in.shape[0]
    first_cos, first_sin = rotation_table(rows, rows, sign)
    last_cos, last_sin = rotation_table(cols, cols, sign)
    grid_real = real_in.reshape(count, rows, cols)
    section_real = jnp.einsum("jm,rmq->rjq", first_cos, grid_real, precision=HIGHEST)
    section_imag = jnp.einsum("jm,rmq->rjq", first_sin, grid_real, precision=HIGHEST)
    if imag_in is not None:
        grid_imag = imag_in.reshape(count, rows, cols)
        section_real = section_real - jnp.einsum(
            "jm,rmq->rjq", first_sin, grid_imag, precision=HIGHEST
        )
        section_imag = section_imag + jnp.einsum(
            "jm,rmq->rjq", first_cos, grid_imag, precision=HIGHEST
        )
    row_index = jnp.arange(rows, dtype=jnp.int32)
    col_index = jnp.arange(cols, dtype=jnp.int32)
    turn = (row_index[:, None] * col_index[None, :] % length).astype(jnp.float32) * (
        2.0 * math.pi / length
    )
    turn_cos = jnp.cos(turn)
    turn_sin = sign * jnp.sin(turn)
    mixed_real = section_real * turn_cos - section_imag * turn_sin
    mixed_imag = section_real * turn_sin + section_imag * turn_cos
    out_real = jnp.einsum("km,rjm->rkj", last_cos, mixed_real, precision=HIGHEST) - jnp.einsum(
        "km,rjm->rkj", last_sin, mixed_imag, precision=HIGHEST
    )
    if real_out:
        return out_real.reshape(count, length)
    out_imag = jnp.einsum("km,rjm->rkj", last_sin, mixed_real, precision=HIGHEST) + jnp.einsum(
        "km,rjm->rkj", last_cos, mixed_imag, precision=HIGHEST
    )
    return (out_real.reshape(count, length), out_imag.reshape(count, length))


def solve_modes(factor, rhs):
    lower_part = lax.linalg.triangular_solve(factor, rhs, left_side=True, lower=True)
    return lax.linalg.triangular_solve(
        factor, lower_part, left_side=True, lower=True, transpose_a=True
    )


def band_of(freq, length, width, bands):
    folded = jnp.minimum(freq, length - freq)
    return jnp.minimum(folded // width, bands - 1)


def pick(array, index):
    return lax.dynamic_index_in_dim(array, index, 0, keepdims=False)


def general_body(tod, pointing, noise_level, modes):
    groups = lax.axis_size("tm")
    row_pos = lax.axis_index("tm")
    det_dev, block = tod.shape
    det_row = det_dev // groups
    length = block * groups
    bands = noise_level.shape[0]
    width = length // groups
    half_block = length // (2 * groups)
    mode_count = modes.shape[2]
    eye = jnp.eye(mode_count, dtype=jnp.float32)
    start = row_pos * half_block
    main_band = band_of(start, length, width, bands)
    side_band = jnp.int32(bands - 1)
    scaled = modes / noise_level[:, :, None]
    partial_all = jnp.einsum("bdm,bdn->bmn", modes, scaled, precision=HIGHEST)
    summed = lax.psum(partial_all, "det")
    gram_main = pick(summed, main_band) + eye
    gram_side = pick(summed, side_band) + eye
    factor_main = jnp.linalg.cholesky(gram_main)
    factor_side = jnp.linalg.cholesky(gram_side)
    arranged = tod.reshape(groups, det_row, block)
    spec_real, spec_imag = transform(
        lax.all_to_all(arranged, "tm", split_axis=0, concat_axis=2, tiled=True)[0],
        None,
        FA,
        FB,
        -1.0,
        False,
    )
    spec_real, spec_imag = (spec_real[None], spec_imag[None])
    spec_real = spec_real[0]
    spec_imag = spec_imag[0]
    basis_main = pick(modes, main_band)
    inverse_main = 1.0 / pick(noise_level, main_band)
    basis_side = pick(modes, side_band)
    inverse_side = 1.0 / pick(noise_level, side_band)
    half = length // 2
    row_noise = lax.dynamic_slice_in_dim(inverse_side, row_pos * det_row, det_row)
    row_basis = lax.dynamic_slice_in_dim(basis_side, row_pos * det_row, det_row, 0)
    top_weighted = spec_real[:, half] * row_noise
    top_proj = jnp.dot(
        top_weighted, row_basis, precision=HIGHEST, preferred_element_type=jnp.float32
    )
    top_proj = lax.psum(top_proj, ("det", "tm"))
    band_real, band_imag = (
        lax.all_to_all(spec_real[:, :half], "tm", split_axis=1, concat_axis=0, tiled=True),
        lax.all_to_all(spec_imag[:, :half], "tm", split_axis=1, concat_axis=0, tiled=True),
    )
    stacked = jnp.concatenate([band_real, band_imag], axis=1) * inverse_main[:, None]
    proj_main = jnp.dot(
        basis_main.T, stacked, precision=HIGHEST, preferred_element_type=jnp.float32
    )
    proj_main = lax.psum(proj_main, "det")
    coef_main = solve_modes(factor_main, proj_main)
    out_main = (
        stacked
        - jnp.dot(basis_main, coef_main, precision=HIGHEST, preferred_element_type=jnp.float32)
        * inverse_main[:, None]
    )
    top_coef = solve_modes(factor_side, top_proj[:, None])[:, 0]
    top_out = (
        top_weighted
        - jnp.dot(row_basis, top_coef, precision=HIGHEST, preferred_element_type=jnp.float32)
        * row_noise
    )
    rows_real, rows_imag = (
        lax.all_to_all(out_main[:, :half_block], "tm", split_axis=0, concat_axis=1, tiled=True),
        lax.all_to_all(out_main[:, half_block:], "tm", split_axis=0, concat_axis=1, tiled=True),
    )
    full_real = jnp.concatenate(
        [rows_real, top_out[:, None], jnp.flip(rows_real[:, 1:], axis=1)], axis=1
    )
    full_imag = jnp.concatenate(
        [rows_imag, jnp.zeros((det_row, 1), jnp.float32), -jnp.flip(rows_imag[:, 1:], axis=1)],
        axis=1,
    )
    filtered_rows = transform(full_real, full_imag, FB, FA, 1.0, True) * (1.0 / length)
    filtered = lax.all_to_all(filtered_rows, "tm", split_axis=1, concat_axis=0, tiled=True)
    pixels = TPIX * lax.axis_size("det") * groups
    flat_pointing = pointing.reshape(-1)
    sums = jax.ops.segment_sum(filtered.reshape(-1), flat_pointing, num_segments=pixels)
    hits = jax.ops.segment_sum(
        jnp.ones(flat_pointing.shape, jnp.float32), flat_pointing, num_segments=pixels
    )
    sums, hits = (
        lax.psum_scatter(sums, ("det", "tm"), scatter_dimension=0, tiled=True),
        lax.psum_scatter(hits, ("det", "tm"), scatter_dimension=0, tiled=True),
    )
    return (filtered, sums / jnp.sqrt(1.0 + hits))


N1 = 128
N2 = 256
CHUNKS = 32
UNROLL = 1
MESH = pl.DeviceIdType.MESH
NT = (((1,), (1,)), ((), ()))
NN = (((1,), (0,)), ((), ()))


def halves(table):
    table = np.asarray(table, np.float32)
    high = table.astype(jnp.bfloat16)
    low = (table - high.astype(np.float32)).astype(jnp.bfloat16)
    return np.stack([np.asarray(high), np.asarray(low)])


def tables():
    length = N1 * N2
    half = N1 // 2
    n1 = np.arange(N1)
    n2 = np.arange(N2)
    k1 = np.arange(half)
    angle = 2 * np.pi * (k1[:, None] * n1[None, :] % N1) / N1
    first = np.concatenate([np.cos(angle), -np.sin(angle)])
    first[half] = np.cos(np.pi * n1)
    turn = 2 * np.pi * (k1[:, None] * n2[None, :]) / length
    tc, ts = np.cos(turn), np.sin(turn)
    t1 = np.concatenate([tc, tc])
    t2 = np.concatenate([ts, -ts])
    t3 = np.concatenate([-ts, -ts])
    t4 = np.concatenate([tc, -tc])
    t1[0], t2[0], t3[0], t4[0] = 1.0, 0.0, 1.0, 0.0
    b = np.pi * n2 / N2
    t1[half], t2[half] = np.cos(b) + np.sin(b), 0.0
    t3[half], t4[half] = np.cos(b) - np.sin(b), 0.0
    twiddle = np.stack([t1, t2, t3, t4]).astype(np.float32)
    angle = 2 * np.pi * (n2[:, None] * n2[None, :] % N2) / N2
    last = np.concatenate([np.cos(angle), np.sin(angle)], axis=1)
    weight = np.full((N1,), 2.0 / length)
    weight[0] = weight[half] = 1.0 / length
    return (
        halves(first),
        twiddle,
        halves(last),
        halves(last.T),
        np.ascontiguousarray(np.swapaxes(twiddle, 1, 2)),
        halves(first.T * weight[None, :]),
    )


def split(x):
    high = x.astype(jnp.bfloat16)
    return high, (x - high.astype(jnp.float32)).astype(jnp.bfloat16)


def dot(a, b, dims):
    return lax.dot_general(a, b, dims, preferred_element_type=jnp.float32)


def dot3(a, b, dims):
    return dot(a[0], b[0], dims) + dot(a[0], b[1], dims) + dot(a[1], b[0], dims)


def eliminate(matrix, begin, end):
    size, lanes = matrix.shape
    row = lax.broadcasted_iota(jnp.int32, (size, lanes), 0)
    lane = lax.broadcasted_iota(jnp.int32, (size, lanes), 1)
    left = lane < size
    column = jnp.where(left, lane, lane - size)

    def step(k, a):
        at_row = row == k
        at_col = column == k
        picked = jnp.where(at_col, a, 0.0)
        one = jnp.sum(jnp.where(left, picked, 0.0), axis=1, keepdims=True)
        two = jnp.sum(jnp.where(left, 0.0, picked), axis=1, keepdims=True)
        c = jnp.where(left, one, two)
        pivot = jnp.sum(jnp.where(at_row, c, 0.0), axis=0, keepdims=True)
        r = jnp.sum(jnp.where(at_row, jnp.where(at_col, 1.0, a), 0.0), axis=0, keepdims=True)
        r = r * (1.0 / pivot)
        base = jnp.where(at_row | at_col, 0.0, a)
        return base - jnp.where(at_row, -1.0, c) * r

    return lax.fori_loop(begin, end, step, matrix)


def expand(matrix):
    size = matrix.shape[0]
    big = size * 8
    spread = (
        lax.broadcasted_iota(jnp.int32, (big, size), 0) // 8
        == lax.broadcasted_iota(jnp.int32, (big, size), 1)
    )
    spread = jnp.where(spread, 1.0, 0.0).astype(jnp.bfloat16)
    same = (
        lax.broadcasted_iota(jnp.int32, (big, big), 0) % 8
        == lax.broadcasted_iota(jnp.int32, (big, big), 1) % 8
    )
    out = []
    for part in split(matrix):
        tall = dot(spread, part, NN).astype(jnp.bfloat16)
        wide = dot(tall, spread, NT)
        out.append(jnp.where(same, wide, 0.0).astype(jnp.bfloat16))
    return out


def fused(
    groups,
    dets,
    tod_ref,
    owner_ref,
    inside_ref,
    mode_ref,
    first_hbm,
    twiddle_hbm,
    last_hbm,
    last_t_hbm,
    twiddle_t_hbm,
    first_t_hbm,
    out_ref,
    map_ref,
    x_in,
    modes_all,
    spec_send,
    spec_recv,
    back_send,
    back_recv,
    time_send,
    kron,
    map_send,
    map_recv,
    first_ref,
    twiddle_ref,
    last_ref,
    last_t_ref,
    twiddle_t_ref,
    first_t_ref,
    masks,
    spots,
    load_sems,
    mode_sems,
    tod_sems,
    spec_sems,
    back_sems,
    time_sems,
    map_sems,
):
    i = lax.axis_index("det")
    t = lax.axis_index("tm")
    total = groups * dets
    me = i * groups + t
    chunk = t * dets + i
    per = mode_ref.shape[1]

    loads = [
        pltpu.make_async_copy(src, dst, load_sems.at[n])
        for n, (src, dst) in enumerate(
            [
                (first_hbm, first_ref),
                (twiddle_hbm, twiddle_ref),
                (last_hbm, last_ref),
                (last_t_hbm, last_t_ref),
                (twiddle_t_hbm, twiddle_t_ref),
                (first_t_hbm, first_t_ref),
            ]
        )
    ]

    def place(p):
        q = p // groups
        return q, p - q * groups

    barrier = pltpu.get_barrier_semaphore()

    def greet(j, carry):
        q, u = place(lax.rem(me + j, total))
        pl.semaphore_signal(barrier, inc=1, device_id=(q, u), device_id_type=MESH)
        return carry

    lax.fori_loop(1, total, greet, 0, unroll=UNROLL)
    for load in loads:
        load.start()
    pl.semaphore_wait(barrier, total - 1)

    def remote(src, dst, sems, j, where):
        return pltpu.make_async_remote_copy(
            src_ref=src,
            dst_ref=dst,
            send_sem=sems.at[0, j],
            recv_sem=sems.at[1, j],
            device_id=where,
            device_id_type=MESH,
        )

    def mode_copy(j):
        rows = pl.ds(pl.multiple_of(i * per, per), per)
        return remote(
            mode_ref, modes_all.at[:, rows, :], mode_sems, j, (lax.rem(i + j, dets), t)
        )

    def tod_copy(j):
        u = lax.rem(t + j, groups)
        rows = pl.ds(pl.multiple_of(t * 16, 16), 16)
        return remote(tod_ref.at[u], x_in.at[:, rows, :], tod_sems, j, (i, u))

    def spec_copy(j):
        q, u = place(lax.rem(me + j, total))
        return remote(spec_send.at[u * dets + q], spec_recv.at[me], spec_sems, j, (q, u))

    def back_copy(j):
        p = lax.rem(me + j, total)
        return remote(back_send.at[p], back_recv.at[chunk], back_sems, j, place(p))

    def time_copy(j):
        u = lax.rem(t + j, groups)
        rows = pl.ds(pl.multiple_of(u * 16, 16), 16)
        return remote(time_send.at[:, rows, :], out_ref.at[t], time_sems, j, (i, u))

    def map_copy(j):
        p = lax.rem(me + j, total)
        return remote(map_send.at[p], map_recv.at[me], map_sems, j, place(p))

    def start_all(make, count):
        def go(j, carry):
            make(j).start()
            return carry

        lax.fori_loop(1, count, go, 0, unroll=UNROLL)

    def wait_all(make, count):
        def go(j, carry):
            make(j).wait()
            return carry

        lax.fori_loop(1, count, go, 0, unroll=UNROLL)

    start_all(mode_copy, dets)
    start_all(tod_copy, groups)

    own_rows = pl.ds(pl.multiple_of(i * per, per), per)
    modes_all[:, own_rows, :] = mode_ref[...]
    x_in[:, pl.ds(pl.multiple_of(t * 16, 16), 16), :] = tod_ref[t]
    for load in loads:
        load.wait()
    wait_all(mode_copy, dets)

    count = modes_all.shape[1]
    square = (count, count)
    diagonal = lax.broadcasted_iota(jnp.int32, square, 0) == lax.broadcasted_iota(
        jnp.int32, square, 1
    )
    sides = []
    for s in range(2):
        basis = modes_all[s, :, :128]
        outer = lax.dot_general(
            basis, basis, NT, precision=HIGHEST, preferred_element_type=jnp.float32
        )
        sides.append(outer + jnp.where(diagonal, modes_all[s, :, 128 : 128 + count], 0.0))
    early = count * 3 // 8
    partial = eliminate(jnp.concatenate(sides, axis=1), 0, early)

    wait_all(tod_copy, groups)
    grid = jnp.concatenate([x_in[0], x_in[1]], axis=1)
    section = dot3((first_ref[0], first_ref[1]), split(grid), NN)
    swapped = jnp.concatenate([section[N1 // 2 :], section[: N1 // 2]], axis=0)
    rows = []
    for d in range(2):
        part = section[:, d * N2 : (d + 1) * N2]
        other = swapped[:, d * N2 : (d + 1) * N2]
        rows.append(
            jnp.concatenate(
                [
                    part * twiddle_ref[0] + other * twiddle_ref[1],
                    part * twiddle_ref[2] + other * twiddle_ref[3],
                ],
                axis=1,
            )
        )
    spectrum = dot3((last_ref[0], last_ref[1]), split(jnp.concatenate(rows, axis=0)), NT)
    for d in range(2):
        spec_send[:, d * 8 : (d + 1) * 8, :] = spectrum[:, d * N1 : (d + 1) * N1].reshape(
            CHUNKS, 8, N1
        )
    start_all(spec_copy, total)
    spec_recv[me] = spec_send[chunk]
    inverse = eliminate(partial, early, count)
    for s in range(2):
        parts = expand(inverse[:, s * count : (s + 1) * count])
        kron[s, 0] = parts[0]
        kron[s, 1] = parts[1]

    wait_all(spec_copy, total)

    data = split(spec_recv[...].reshape(total * 16, N1))
    main = dot3((kron[0, 0], kron[0, 1]), data, NN)
    side = dot3((kron[1, 0], kron[1, 1]), data, NN)
    shape = (total * 16, N1)
    edge = (lax.broadcasted_iota(jnp.int32, shape, 0) % 8 == 0) & (
        lax.broadcasted_iota(jnp.int32, shape, 1) == 0
    )
    apart = jnp.where((t > groups // 2) & (i == 0), 1, 0)
    edge = edge & (jnp.full(shape, apart, jnp.int32) == 1)
    back_send[...] = jnp.where(edge, side, main).reshape(total, 16, N1)
    start_all(back_copy, total)
    back_recv[chunk] = back_send[me]

    width = 8 * N2
    own_index = lax.broadcasted_iota(jnp.int32, (total, width), 0)
    inside_index = lax.broadcasted_iota(jnp.int32, (TPIX, width), 0)

    def flat(block):
        return jnp.concatenate([block[r : r + 1] for r in range(8)], axis=1)

    def mark(g, acc):
        a = g // 4
        b = g - a * 4
        c = b // 2
        rows = pl.ds(pl.multiple_of((b - c * 2) * 8, 8), 8)
        mine = jnp.broadcast_to(flat(owner_ref[a, c, rows, :]), (total, width)) == own_index
        spot = jnp.broadcast_to(flat(inside_ref[a, c, rows, :]), (TPIX, width)) == inside_index
        mine = jnp.where(mine, 1.0, 0.0).astype(jnp.bfloat16)
        spot = jnp.where(spot, 1.0, 0.0).astype(jnp.bfloat16)
        masks[g] = mine
        spots[g] = spot
        return acc + dot(mine, spot, NT)

    hits = lax.fori_loop(0, 4 * groups, mark, jnp.zeros((total, TPIX), jnp.float32))
    wait_all(back_copy, total)

    weighted = jnp.concatenate(
        [back_recv[:, d * 8 : (d + 1) * 8, :].reshape(N2, N1) for d in range(2)], axis=1
    )
    spread = dot3((last_t_ref[0], last_t_ref[1]), split(weighted), NN)
    upright = []
    for d in range(2):
        p = spread[:N2, d * N1 : (d + 1) * N1]
        q = spread[N2:, d * N1 : (d + 1) * N1]
        crossed = p * twiddle_t_ref[1] + q * twiddle_t_ref[3]
        upright.append(
            p * twiddle_t_ref[0]
            + q * twiddle_t_ref[2]
            + jnp.concatenate([crossed[:, N1 // 2 :], crossed[:, : N1 // 2]], axis=1)
        )
    stamped = dot3(
        (first_t_ref[0], first_t_ref[1]), split(jnp.concatenate(upright, axis=0)), NT
    )
    for d in range(2):
        time_send[d] = stamped[:, d * N2 : (d + 1) * N2]
    start_all(time_copy, groups)
    out_ref[t] = time_send[:, pl.ds(pl.multiple_of(t * 16, 16), 16), :]

    def bin_block(a, acc):
        for b in range(4):
            values = out_ref[a, b // 2, b % 2 * 8 : b % 2 * 8 + 8, :]
            high, low = split(flat(values))
            mine = masks[a * 4 + b]
            lhs = jnp.concatenate(
                [
                    mine * jnp.broadcast_to(high, (total, width)),
                    mine * jnp.broadcast_to(low, (total, width)),
                ],
                axis=0,
            )
            acc = acc + dot(lhs, spots[a * 4 + b], NT)
        return acc

    def bin_arrived(j, acc):
        time_copy(j).wait()
        return bin_block(lax.rem(t - j + groups, groups), acc)

    acc = bin_block(t, jnp.zeros((2 * total, TPIX), jnp.float32))
    acc = lax.fori_loop(1, groups, bin_arrived, acc)
    pad = jnp.zeros((total, 128 - TPIX), jnp.float32)
    map_send[...] = jnp.zeros(map_send.shape, jnp.float32)
    map_send[:, 0, :] = jnp.concatenate([acc[:total] + acc[total:], pad], axis=1)
    map_send[:, 1, :] = jnp.concatenate([hits, pad], axis=1)
    start_all(map_copy, total)
    map_recv[me] = map_send[me]
    wait_all(map_copy, total)
    summed = jnp.sum(map_recv[...], axis=0)
    map_ref[...] = jnp.broadcast_to(summed[0:1] / jnp.sqrt(1.0 + summed[1:2]), map_ref.shape)


def fast_body(tod, pointing, noise_level, modes):
    groups = lax.axis_size("tm")
    dets = lax.axis_size("det")
    t = lax.axis_index("tm")
    det_dev = tod.shape[0]
    bands = noise_level.shape[0]
    total = groups * dets
    main_band = jnp.minimum(t, groups - 1 - t)
    side_band = jnp.minimum(main_band + 1, bands - 1)
    blocks = (groups, det_dev // groups, 16, N2)
    owner = (pointing // TPIX).reshape(blocks)
    inside = (pointing % TPIX).reshape(blocks)
    pair_modes = jnp.stack([pick(modes, main_band), pick(modes, side_band)])
    pair_noise = jnp.stack([pick(noise_level, main_band), pick(noise_level, side_band)])
    pair_noise = jnp.broadcast_to(pair_noise[:, :, None], pair_modes.shape)
    pair = jnp.concatenate([pair_modes, pair_noise], axis=2)
    everyone = det_dev * dets
    f32 = jnp.float32
    constants = [jnp.asarray(c) for c in tables()]
    vmem = pl.BlockSpec(memory_space=pltpu.VMEM)
    out, binned = pl.pallas_call(
        functools.partial(fused, groups, dets),
        out_shape=(
            jax.ShapeDtypeStruct(blocks, f32),
            jax.ShapeDtypeStruct((8, 128), f32),
        ),
        in_specs=[vmem] * 4 + [pl.BlockSpec(memory_space=pltpu.HBM)] * len(constants),
        out_specs=(vmem, vmem),
        scratch_shapes=[
            pltpu.VMEM((2, N1, N2), f32),
            pltpu.VMEM((2, everyone, 256), f32),
            pltpu.VMEM((total, 16, 128), f32),
            pltpu.VMEM((total, 16, 128), f32),
            pltpu.VMEM((total, 16, 128), f32),
            pltpu.VMEM((total, 16, 128), f32),
            pltpu.VMEM((2, N1, N2), f32),
            pltpu.VMEM((2, 2, everyone * 8, everyone * 8), jnp.bfloat16),
            pltpu.VMEM((total, 2, 128), f32),
            pltpu.VMEM((total, 2, 128), f32),
            *[pltpu.VMEM(c.shape, c.dtype) for c in constants],
            pltpu.VMEM((4 * groups, total, 8 * N2), jnp.bfloat16),
            pltpu.VMEM((4 * groups, TPIX, 8 * N2), jnp.bfloat16),
            pltpu.SemaphoreType.DMA((len(constants),)),
            pltpu.SemaphoreType.DMA((2, dets)),
            pltpu.SemaphoreType.DMA((2, groups)),
            pltpu.SemaphoreType.DMA((2, total)),
            pltpu.SemaphoreType.DMA((2, total)),
            pltpu.SemaphoreType.DMA((2, groups)),
            pltpu.SemaphoreType.DMA((2, total)),
        ],
        compiler_params=pltpu.CompilerParams(
            collective_id=0, has_side_effects=True, vmem_limit_bytes=40 * 1024 * 1024
        ),
    )(tod.reshape(blocks), owner, inside, pair, *constants)
    return out.reshape(tod.shape), binned[0, :TPIX]


def body(tod, pointing, noise_level, modes):
    groups = lax.axis_size("tm")
    dets = lax.axis_size("det")
    fits = (
        groups * dets == CHUNKS
        and groups == 2 * noise_level.shape[0]
        and tod.shape == (2 * groups, N1 * N2 // groups)
        and modes.shape[2] == 128
        and 16 * groups == N1
    )
    return (fast_body if fits else general_body)(tod, pointing, noise_level, modes)


def solution(mesh):
    placed = (P("det", "tm"), P("det", "tm"), P(None, "det"), P(None, "det", None))
    return jax.shard_map(
        body,
        mesh=mesh,
        in_specs=placed,
        out_specs=(P("det", "tm"), P(("det", "tm"))),
        check_vma=False,
    )
```

```python
import functools
import math

import jax
import jax.numpy as jnp
import numpy as np
from jax import lax
from jax.experimental import pallas as pl
from jax.experimental.pallas import tpu as pltpu
from jax.sharding import PartitionSpec as P

FA = 128
FB = 256
TPIX = 48


HIGHEST = lax.Precision.HIGHEST


def rotation_table(size, total, sign):
    index = jnp.arange(size, dtype=jnp.int32)
    product = index[:, None] * index[None, :] % total
    angle = 2.0 * math.pi / total * product.astype(jnp.float32)
    return (jnp.cos(angle), sign * jnp.sin(angle))


def transform(real_in, imag_in, rows, cols, sign, real_out):
    length = rows * cols
    count = real_in.shape[0]
    first_cos, first_sin = rotation_table(rows, rows, sign)
    last_cos, last_sin = rotation_table(cols, cols, sign)
    grid_real = real_in.reshape(count, rows, cols)
    section_real = jnp.einsum("jm,rmq->rjq", first_cos, grid_real, precision=HIGHEST)
    section_imag = jnp.einsum("jm,rmq->rjq", first_sin, grid_real, precision=HIGHEST)
    if imag_in is not None:
        grid_imag = imag_in.reshape(count, rows, cols)
        section_real = section_real - jnp.einsum(
            "jm,rmq->rjq", first_sin, grid_imag, precision=HIGHEST
        )
        section_imag = section_imag + jnp.einsum(
            "jm,rmq->rjq", first_cos, grid_imag, precision=HIGHEST
        )
    row_index = jnp.arange(rows, dtype=jnp.int32)
    col_index = jnp.arange(cols, dtype=jnp.int32)
    turn = (row_index[:, None] * col_index[None, :] % length).astype(jnp.float32) * (
        2.0 * math.pi / length
    )
    turn_cos = jnp.cos(turn)
    turn_sin = sign * jnp.sin(turn)
    mixed_real = section_real * turn_cos - section_imag * turn_sin
    mixed_imag = section_real * turn_sin + section_imag * turn_cos
    out_real = jnp.einsum("km,rjm->rkj", last_cos, mixed_real, precision=HIGHEST) - jnp.einsum(
        "km,rjm->rkj", last_sin, mixed_imag, precision=HIGHEST
    )
    if real_out:
        return out_real.reshape(count, length)
    out_imag = jnp.einsum("km,rjm->rkj", last_sin, mixed_real, precision=HIGHEST) + jnp.einsum(
        "km,rjm->rkj", last_cos, mixed_imag, precision=HIGHEST
    )
    return (out_real.reshape(count, length), out_imag.reshape(count, length))


def solve_modes(factor, rhs):
    lower_part = lax.linalg.triangular_solve(factor, rhs, left_side=True, lower=True)
    return lax.linalg.triangular_solve(
        factor, lower_part, left_side=True, lower=True, transpose_a=True
    )


def band_of(freq, length, width, bands):
    folded = jnp.minimum(freq, length - freq)
    return jnp.minimum(folded // width, bands - 1)


def pick(array, index):
    return lax.dynamic_index_in_dim(array, index, 0, keepdims=False)


def general_body(tod, pointing, noise_level, modes):
    groups = lax.axis_size("tm")
    row_pos = lax.axis_index("tm")
    det_dev, block = tod.shape
    det_row = det_dev // groups
    length = block * groups
    bands = noise_level.shape[0]
    width = length // groups
    half_block = length // (2 * groups)
    mode_count = modes.shape[2]
    eye = jnp.eye(mode_count, dtype=jnp.float32)
    start = row_pos * half_block
    main_band = band_of(start, length, width, bands)
    side_band = jnp.int32(bands - 1)
    scaled = modes / noise_level[:, :, None]
    partial_all = jnp.einsum("bdm,bdn->bmn", modes, scaled, precision=HIGHEST)
    summed = lax.psum(partial_all, "det")
    gram_main = pick(summed, main_band) + eye
    gram_side = pick(summed, side_band) + eye
    factor_main = jnp.linalg.cholesky(gram_main)
    factor_side = jnp.linalg.cholesky(gram_side)
    arranged = tod.reshape(groups, det_row, block)
    spec_real, spec_imag = transform(
        lax.all_to_all(arranged, "tm", split_axis=0, concat_axis=2, tiled=True)[0],
        None,
        FA,
        FB,
        -1.0,
        False,
    )
    spec_real, spec_imag = (spec_real[None], spec_imag[None])
    spec_real = spec_real[0]
    spec_imag = spec_imag[0]
    basis_main = pick(modes, main_band)
    inverse_main = 1.0 / pick(noise_level, main_band)
    basis_side = pick(modes, side_band)
    inverse_side = 1.0 / pick(noise_level, side_band)
    half = length // 2
    row_noise = lax.dynamic_slice_in_dim(inverse_side, row_pos * det_row, det_row)
    row_basis = lax.dynamic_slice_in_dim(basis_side, row_pos * det_row, det_row, 0)
    top_weighted = spec_real[:, half] * row_noise
    top_proj = jnp.dot(
        top_weighted, row_basis, precision=HIGHEST, preferred_element_type=jnp.float32
    )
    top_proj = lax.psum(top_proj, ("det", "tm"))
    band_real, band_imag = (
        lax.all_to_all(spec_real[:, :half], "tm", split_axis=1, concat_axis=0, tiled=True),
        lax.all_to_all(spec_imag[:, :half], "tm", split_axis=1, concat_axis=0, tiled=True),
    )
    stacked = jnp.concatenate([band_real, band_imag], axis=1) * inverse_main[:, None]
    proj_main = jnp.dot(
        basis_main.T, stacked, precision=HIGHEST, preferred_element_type=jnp.float32
    )
    proj_main = lax.psum(proj_main, "det")
    coef_main = solve_modes(factor_main, proj_main)
    out_main = (
        stacked
        - jnp.dot(basis_main, coef_main, precision=HIGHEST, preferred_element_type=jnp.float32)
        * inverse_main[:, None]
    )
    top_coef = solve_modes(factor_side, top_proj[:, None])[:, 0]
    top_out = (
        top_weighted
        - jnp.dot(row_basis, top_coef, precision=HIGHEST, preferred_element_type=jnp.float32)
        * row_noise
    )
    rows_real, rows_imag = (
        lax.all_to_all(out_main[:, :half_block], "tm", split_axis=0, concat_axis=1, tiled=True),
        lax.all_to_all(out_main[:, half_block:], "tm", split_axis=0, concat_axis=1, tiled=True),
    )
    full_real = jnp.concatenate(
        [rows_real, top_out[:, None], jnp.flip(rows_real[:, 1:], axis=1)], axis=1
    )
    full_imag = jnp.concatenate(
        [rows_imag, jnp.zeros((det_row, 1), jnp.float32), -jnp.flip(rows_imag[:, 1:], axis=1)],
        axis=1,
    )
    filtered_rows = transform(full_real, full_imag, FB, FA, 1.0, True) * (1.0 / length)
    filtered = lax.all_to_all(filtered_rows, "tm", split_axis=1, concat_axis=0, tiled=True)
    pixels = TPIX * lax.axis_size("det") * groups
    flat_pointing = pointing.reshape(-1)
    sums = jax.ops.segment_sum(filtered.reshape(-1), flat_pointing, num_segments=pixels)
    hits = jax.ops.segment_sum(
        jnp.ones(flat_pointing.shape, jnp.float32), flat_pointing, num_segments=pixels
    )
    sums, hits = (
        lax.psum_scatter(sums, ("det", "tm"), scatter_dimension=0, tiled=True),
        lax.psum_scatter(hits, ("det", "tm"), scatter_dimension=0, tiled=True),
    )
    return (filtered, sums / jnp.sqrt(1.0 + hits))


N1 = 128
N2 = 256
CHUNKS = 32
UNROLL = True
MESH = pl.DeviceIdType.MESH
NT = (((1,), (1,)), ((), ()))
NN = (((1,), (0,)), ((), ()))


def halves(table):
    table = np.asarray(table, np.float32)
    high = table.astype(jnp.bfloat16)
    low = (table - high.astype(np.float32)).astype(jnp.bfloat16)
    return np.stack([np.asarray(high), np.asarray(low)])


def tables():
    length = N1 * N2
    half = N1 // 2
    n1 = np.arange(N1)
    n2 = np.arange(N2)
    k1 = np.arange(half)
    angle = 2 * np.pi * (k1[:, None] * n1[None, :] % N1) / N1
    first = np.concatenate([np.cos(angle), -np.sin(angle)])
    first[half] = np.cos(np.pi * n1)
    turn = 2 * np.pi * (k1[:, None] * n2[None, :]) / length
    tc, ts = np.cos(turn), np.sin(turn)
    t1 = np.concatenate([tc, tc])
    t2 = np.concatenate([ts, -ts])
    t3 = np.concatenate([-ts, -ts])
    t4 = np.concatenate([tc, -tc])
    t1[0], t2[0], t3[0], t4[0] = 1.0, 0.0, 1.0, 0.0
    b = np.pi * n2 / N2
    t1[half], t2[half] = np.cos(b) + np.sin(b), 0.0
    t3[half], t4[half] = np.cos(b) - np.sin(b), 0.0
    twiddle = np.stack([t1, t2, t3, t4]).astype(np.float32)
    angle = 2 * np.pi * (n2[:, None] * n2[None, :] % N2) / N2
    last = np.concatenate([np.cos(angle), np.sin(angle)], axis=1)
    weight = np.full((N1,), 2.0 / length)
    weight[0] = weight[half] = 1.0 / length
    return (
        halves(first),
        twiddle,
        halves(last),
        halves(last.T),
        np.ascontiguousarray(np.swapaxes(twiddle, 1, 2)),
        halves(first.T * weight[None, :]),
    )


def split(x):
    high = x.astype(jnp.bfloat16)
    return high, (x - high.astype(jnp.float32)).astype(jnp.bfloat16)


def dot(a, b, dims):
    return lax.dot_general(a, b, dims, preferred_element_type=jnp.float32)


def dot3(a, b, dims):
    return dot(a[0], b[0], dims) + dot(a[0], b[1], dims) + dot(a[1], b[0], dims)


def eliminate(matrix, begin, end):
    size, lanes = matrix.shape
    row = lax.broadcasted_iota(jnp.int32, (size, lanes), 0)
    lane = lax.broadcasted_iota(jnp.int32, (size, lanes), 1)
    left = lane < size
    column = jnp.where(left, lane, lane - size)

    def step(k, a):
        at_row = row == k
        at_col = column == k
        picked = jnp.where(at_col, a, 0.0)
        one = jnp.sum(jnp.where(left, picked, 0.0), axis=1, keepdims=True)
        two = jnp.sum(jnp.where(left, 0.0, picked), axis=1, keepdims=True)
        c = jnp.where(left, one, two)
        pivot = jnp.sum(jnp.where(at_row, c, 0.0), axis=0, keepdims=True)
        r = jnp.sum(jnp.where(at_row, jnp.where(at_col, 1.0, a), 0.0), axis=0, keepdims=True)
        r = r * (1.0 / pivot)
        base = jnp.where(at_row | at_col, 0.0, a)
        return base - jnp.where(at_row, -1.0, c) * r

    return lax.fori_loop(begin, end, step, matrix)


def expand(matrix):
    size = matrix.shape[0]
    big = size * 8
    spread = (
        lax.broadcasted_iota(jnp.int32, (big, size), 0) // 8
        == lax.broadcasted_iota(jnp.int32, (big, size), 1)
    )
    spread = jnp.where(spread, 1.0, 0.0).astype(jnp.bfloat16)
    same = (
        lax.broadcasted_iota(jnp.int32, (big, big), 0) % 8
        == lax.broadcasted_iota(jnp.int32, (big, big), 1) % 8
    )
    out = []
    for part in split(matrix):
        tall = dot(spread, part, NN).astype(jnp.bfloat16)
        wide = dot(tall, spread, NT)
        out.append(jnp.where(same, wide, 0.0).astype(jnp.bfloat16))
    return out


def fused(
    groups,
    dets,
    tod_ref,
    owner_ref,
    inside_ref,
    mode_ref,
    first_hbm,
    twiddle_hbm,
    last_hbm,
    last_t_hbm,
    twiddle_t_hbm,
    first_t_hbm,
    out_ref,
    map_ref,
    x_in,
    modes_all,
    spec_send,
    spec_recv,
    back_send,
    back_recv,
    time_send,
    kron,
    map_send,
    map_recv,
    first_ref,
    twiddle_ref,
    last_ref,
    last_t_ref,
    twiddle_t_ref,
    first_t_ref,
    masks,
    spots,
    load_sems,
    mode_sems,
    tod_sems,
    spec_sems,
    back_sems,
    time_sems,
    map_sems,
):
    i = lax.axis_index("det")
    t = lax.axis_index("tm")
    total = groups * dets
    me = i * groups + t
    chunk = t * dets + i
    per = mode_ref.shape[1]

    loads = [
        pltpu.make_async_copy(src, dst, load_sems.at[n])
        for n, (src, dst) in enumerate(
            [
                (first_hbm, first_ref),
                (twiddle_hbm, twiddle_ref),
                (last_hbm, last_ref),
                (last_t_hbm, last_t_ref),
                (twiddle_t_hbm, twiddle_t_ref),
                (first_t_hbm, first_t_ref),
            ]
        )
    ]

    def place(p):
        q = p // groups
        return q, p - q * groups

    barrier = pltpu.get_barrier_semaphore()

    def greet(j, carry):
        q, u = place(lax.rem(me + j, total))
        pl.semaphore_signal(barrier, inc=1, device_id=(q, u), device_id_type=MESH)
        return carry

    lax.fori_loop(1, total, greet, 0, unroll=UNROLL)
    for load in loads:
        load.start()
    pl.semaphore_wait(barrier, total - 1)

    def remote(src, dst, sems, j, where):
        return pltpu.make_async_remote_copy(
            src_ref=src,
            dst_ref=dst,
            send_sem=sems.at[0, j],
            recv_sem=sems.at[1, j],
            device_id=where,
            device_id_type=MESH,
        )

    def mode_copy(j):
        rows = pl.ds(pl.multiple_of(i * per, per), per)
        return remote(
            mode_ref, modes_all.at[:, rows, :], mode_sems, j, (lax.rem(i + j, dets), t)
        )

    def tod_copy(j):
        u = lax.rem(t + j, groups)
        rows = pl.ds(pl.multiple_of(t * 16, 16), 16)
        return remote(tod_ref.at[u], x_in.at[:, rows, :], tod_sems, j, (i, u))

    def spec_copy(j):
        q, u = place(lax.rem(me + j, total))
        return remote(spec_send.at[u * dets + q], spec_recv.at[me], spec_sems, j, (q, u))

    def back_copy(j):
        p = lax.rem(me + j, total)
        return remote(back_send.at[p], back_recv.at[chunk], back_sems, j, place(p))

    def time_copy(j):
        u = lax.rem(t + j, groups)
        rows = pl.ds(pl.multiple_of(u * 16, 16), 16)
        return remote(time_send.at[:, rows, :], out_ref.at[t], time_sems, j, (i, u))

    def map_copy(j):
        p = lax.rem(me + j, total)
        return remote(map_send.at[p], map_recv.at[me], map_sems, j, place(p))

    def start_all(make, count):
        def go(j, carry):
            make(j).start()
            return carry

        lax.fori_loop(1, count, go, 0, unroll=UNROLL)

    def wait_all(make, count):
        def go(j, carry):
            make(j).wait()
            return carry

        lax.fori_loop(1, count, go, 0, unroll=UNROLL)

    start_all(mode_copy, dets)
    start_all(tod_copy, groups)

    own_rows = pl.ds(pl.multiple_of(i * per, per), per)
    modes_all[:, own_rows, :] = mode_ref[...]
    x_in[:, pl.ds(pl.multiple_of(t * 16, 16), 16), :] = tod_ref[t]
    for load in loads:
        load.wait()
    wait_all(mode_copy, dets)

    count = modes_all.shape[1]
    square = (count, count)
    diagonal = lax.broadcasted_iota(jnp.int32, square, 0) == lax.broadcasted_iota(
        jnp.int32, square, 1
    )
    sides = []
    for s in range(2):
        basis = modes_all[s, :, :128]
        outer = lax.dot_general(
            basis, basis, NT, precision=HIGHEST, preferred_element_type=jnp.float32
        )
        sides.append(outer + jnp.where(diagonal, modes_all[s, :, 128 : 128 + count], 0.0))
    early = count * 3 // 8
    partial = eliminate(jnp.concatenate(sides, axis=1), 0, early)

    wait_all(tod_copy, groups)
    grid = jnp.concatenate([x_in[0], x_in[1]], axis=1)
    section = dot3((first_ref[0], first_ref[1]), split(grid), NN)
    swapped = jnp.concatenate([section[N1 // 2 :], section[: N1 // 2]], axis=0)
    rows = []
    for d in range(2):
        part = section[:, d * N2 : (d + 1) * N2]
        other = swapped[:, d * N2 : (d + 1) * N2]
        rows.append(
            jnp.concatenate(
                [
                    part * twiddle_ref[0] + other * twiddle_ref[1],
                    part * twiddle_ref[2] + other * twiddle_ref[3],
                ],
                axis=1,
            )
        )
    spectrum = dot3((last_ref[0], last_ref[1]), split(jnp.concatenate(rows, axis=0)), NT)
    for d in range(2):
        spec_send[:, d * 8 : (d + 1) * 8, :] = spectrum[:, d * N1 : (d + 1) * N1].reshape(
            CHUNKS, 8, N1
        )
    start_all(spec_copy, total)
    spec_recv[me] = spec_send[chunk]
    inverse = eliminate(partial, early, count)
    for s in range(2):
        parts = expand(inverse[:, s * count : (s + 1) * count])
        kron[s, 0] = parts[0]
        kron[s, 1] = parts[1]

    wait_all(spec_copy, total)

    data = split(spec_recv[...].reshape(total * 16, N1))
    main = dot3((kron[0, 0], kron[0, 1]), data, NN)
    side = dot3((kron[1, 0], kron[1, 1]), data, NN)
    shape = (total * 16, N1)
    edge = (lax.broadcasted_iota(jnp.int32, shape, 0) % 8 == 0) & (
        lax.broadcasted_iota(jnp.int32, shape, 1) == 0
    )
    apart = jnp.where((t > groups // 2) & (i == 0), 1, 0)
    edge = edge & (jnp.full(shape, apart, jnp.int32) == 1)
    back_send[...] = jnp.where(edge, side, main).reshape(total, 16, N1)
    start_all(back_copy, total)
    back_recv[chunk] = back_send[me]

    width = 8 * N2
    own_index = lax.broadcasted_iota(jnp.int32, (total, width), 0)
    inside_index = lax.broadcasted_iota(jnp.int32, (TPIX, width), 0)

    def flat(block):
        return jnp.concatenate([block[r : r + 1] for r in range(8)], axis=1)

    def mark(g, acc):
        a = g // 4
        b = g - a * 4
        c = b // 2
        rows = pl.ds(pl.multiple_of((b - c * 2) * 8, 8), 8)
        mine = jnp.broadcast_to(flat(owner_ref[a, c, rows, :]), (total, width)) == own_index
        spot = jnp.broadcast_to(flat(inside_ref[a, c, rows, :]), (TPIX, width)) == inside_index
        mine = jnp.where(mine, 1.0, 0.0).astype(jnp.bfloat16)
        spot = jnp.where(spot, 1.0, 0.0).astype(jnp.bfloat16)
        masks[g] = mine
        spots[g] = spot
        return acc + dot(mine, spot, NT)

    hits = lax.fori_loop(0, 4 * groups, mark, jnp.zeros((total, TPIX), jnp.float32))
    wait_all(back_copy, total)

    weighted = jnp.concatenate(
        [back_recv[:, d * 8 : (d + 1) * 8, :].reshape(N2, N1) for d in range(2)], axis=1
    )
    spread = dot3((last_t_ref[0], last_t_ref[1]), split(weighted), NN)
    upright = []
    for d in range(2):
        p = spread[:N2, d * N1 : (d + 1) * N1]
        q = spread[N2:, d * N1 : (d + 1) * N1]
        crossed = p * twiddle_t_ref[1] + q * twiddle_t_ref[3]
        upright.append(
            p * twiddle_t_ref[0]
            + q * twiddle_t_ref[2]
            + jnp.concatenate([crossed[:, N1 // 2 :], crossed[:, : N1 // 2]], axis=1)
        )
    stamped = dot3(
        (first_t_ref[0], first_t_ref[1]), split(jnp.concatenate(upright, axis=0)), NT
    )
    for d in range(2):
        time_send[d] = stamped[:, d * N2 : (d + 1) * N2]
    start_all(time_copy, groups)
    out_ref[t] = time_send[:, pl.ds(pl.multiple_of(t * 16, 16), 16), :]

    def bin_block(a, acc):
        for b in range(4):
            values = out_ref[a, b // 2, b % 2 * 8 : b % 2 * 8 + 8, :]
            high, low = split(flat(values))
            mine = masks[a * 4 + b]
            lhs = jnp.concatenate(
                [
                    mine * jnp.broadcast_to(high, (total, width)),
                    mine * jnp.broadcast_to(low, (total, width)),
                ],
                axis=0,
            )
            acc = acc + dot(lhs, spots[a * 4 + b], NT)
        return acc

    def bin_arrived(j, acc):
        time_copy(j).wait()
        return bin_block(lax.rem(t - j + groups, groups), acc)

    acc = bin_block(t, jnp.zeros((2 * total, TPIX), jnp.float32))
    acc = lax.fori_loop(1, groups, bin_arrived, acc)
    pad = jnp.zeros((total, 128 - TPIX), jnp.float32)
    map_send[...] = jnp.zeros(map_send.shape, jnp.float32)
    map_send[:, 0, :] = jnp.concatenate([acc[:total] + acc[total:], pad], axis=1)
    map_send[:, 1, :] = jnp.concatenate([hits, pad], axis=1)
    start_all(map_copy, total)
    map_recv[me] = map_send[me]
    wait_all(map_copy, total)
    summed = jnp.sum(map_recv[...], axis=0)
    map_ref[...] = jnp.broadcast_to(summed[0:1] / jnp.sqrt(1.0 + summed[1:2]), map_ref.shape)


def fast_body(tod, pointing, noise_level, modes):
    groups = lax.axis_size("tm")
    dets = lax.axis_size("det")
    t = lax.axis_index("tm")
    det_dev = tod.shape[0]
    bands = noise_level.shape[0]
    total = groups * dets
    main_band = jnp.minimum(t, groups - 1 - t)
    side_band = jnp.minimum(main_band + 1, bands - 1)
    blocks = (groups, det_dev // groups, 16, N2)
    owner = (pointing // TPIX).reshape(blocks)
    inside = (pointing % TPIX).reshape(blocks)
    pair_modes = jnp.stack([pick(modes, main_band), pick(modes, side_band)])
    pair_noise = jnp.stack([pick(noise_level, main_band), pick(noise_level, side_band)])
    pair_noise = jnp.broadcast_to(pair_noise[:, :, None], pair_modes.shape)
    pair = jnp.concatenate([pair_modes, pair_noise], axis=2)
    everyone = det_dev * dets
    f32 = jnp.float32
    constants = [jnp.asarray(c) for c in tables()]
    vmem = pl.BlockSpec(memory_space=pltpu.VMEM)
    out, binned = pl.pallas_call(
        functools.partial(fused, groups, dets),
        out_shape=(
            jax.ShapeDtypeStruct(blocks, f32),
            jax.ShapeDtypeStruct((8, 128), f32),
        ),
        in_specs=[vmem] * 4 + [pl.BlockSpec(memory_space=pltpu.HBM)] * len(constants),
        out_specs=(vmem, vmem),
        scratch_shapes=[
            pltpu.VMEM((2, N1, N2), f32),
            pltpu.VMEM((2, everyone, 256), f32),
            pltpu.VMEM((total, 16, 128), f32),
            pltpu.VMEM((total, 16, 128), f32),
            pltpu.VMEM((total, 16, 128), f32),
            pltpu.VMEM((total, 16, 128), f32),
            pltpu.VMEM((2, N1, N2), f32),
            pltpu.VMEM((2, 2, everyone * 8, everyone * 8), jnp.bfloat16),
            pltpu.VMEM((total, 2, 128), f32),
            pltpu.VMEM((total, 2, 128), f32),
            *[pltpu.VMEM(c.shape, c.dtype) for c in constants],
            pltpu.VMEM((4 * groups, total, 8 * N2), jnp.bfloat16),
            pltpu.VMEM((4 * groups, TPIX, 8 * N2), jnp.bfloat16),
            pltpu.SemaphoreType.DMA((len(constants),)),
            pltpu.SemaphoreType.DMA((2, dets)),
            pltpu.SemaphoreType.DMA((2, groups)),
            pltpu.SemaphoreType.DMA((2, total)),
            pltpu.SemaphoreType.DMA((2, total)),
            pltpu.SemaphoreType.DMA((2, groups)),
            pltpu.SemaphoreType.DMA((2, total)),
        ],
        compiler_params=pltpu.CompilerParams(
            collective_id=0, has_side_effects=True, vmem_limit_bytes=40 * 1024 * 1024
        ),
    )(tod.reshape(blocks), owner, inside, pair, *constants)
    return out.reshape(tod.shape), binned[0, :TPIX]


def body(tod, pointing, noise_level, modes):
    groups = lax.axis_size("tm")
    dets = lax.axis_size("det")
    fits = (
        groups * dets == CHUNKS
        and groups == 2 * noise_level.shape[0]
        and tod.shape == (2 * groups, N1 * N2 // groups)
        and modes.shape[2] == 128
        and 16 * groups == N1
    )
    return (fast_body if fits else general_body)(tod, pointing, noise_level, modes)


def solution(mesh):
    placed = (P("det", "tm"), P("det", "tm"), P(None, "det"), P(None, "det", None))
    return jax.shard_map(
        body,
        mesh=mesh,
        in_specs=placed,
        out_specs=(P("det", "tm"), P(("det", "tm"))),
        check_vma=False,
    )
```
